256 devices in a mesh: ta: 8 (over z), ha: 32 (over x, y, core).
Axes of the slice: x: 4, y: 4, z: 8, core: 2. Of those that a mesh axis runs over, the one named last changes fastest.
Arguments:
- mode_record: bfloat16 [300, 16384], P(None, ('ta', 'ha')), may hold values from -18 to 18
- mode_shapes: bfloat16 [300, 12288], P(None, 'ha'), may hold values from -2.5 to 2.5
- map_elem: int32 [4, 16384], P(None, 'ha'), may hold values from 0 to 383
- map_coef: float32 [4, 16384], P(None, 'ha'), may hold values from -3 to 3
- hot_owner: int32 [8192], P(('ta', 'ha')), may hold values from 0 to 31, as said below
- band_bins: int32 [512], replicated, may hold values from 1 to 64, 8192 in all
Outputs:
- elem_rms: float32 [12288], P('ha')
- band_power: float32 [8192, 512], P(('ta', 'ha'))
The draws below stay inside these ranges and needn't reach their ends.
Inputs may be any that keep to these rules, and one draw needn't show every extreme that they name: hot_owner[h] is the region whose map slots describe hotspot h. In each aligned block of 32 hotspots (the hotspots of one device) no region owns more than 2, and one region, the same for every block, owns exactly 2 of each block. `map_elem`: slots that no hotspot's map slot names are never read. `band_bins`: the bands follow each other from bin 0 and together cover the 8192 bins below the Nyquist bin.
All inputs are finite; a program needn't handle non-finite values.
Results may differ from the reference program's by a relative error of at most 0.004.
Values may be sent and summed in bfloat16 or wider, within the bound.
A program may use at most 64 MiB of HBM per device.

```python
import math
import jax
import jax.numpy as jnp
import numpy as np
from jax import lax

M = 300
DFT_LEN = 128
NB = 512
K_EXT = 4
MOST_BINS = 64
E_DEV = 384
HS_DEV = 32
NT = 16384
NE = 12288
NH = 8192
CAPB = 2
HOT_CAP = 512
N_TA = 8
N_HA = 32


def draw_mode_record(key, part):
    key = jax.random.fold_in(key, 3)
    key_scale, key_noise, key_common = jax.random.split(key, 3)
    steps = jnp.arange(NT, dtype=jnp.int32)
    fraction = steps.astype(jnp.float32) / NT
    parity = jnp.where(steps % 2 == 1, 0.5, 1.0).astype(jnp.float32)
    mode_scale = 10.0 ** (-jax.random.uniform(key_scale, (M, 1)))
    own_draw = jax.random.truncated_normal(key_noise, -4.0, 4.0, (M, NT))
    common_draw = jax.random.truncated_normal(key_common, -4.0, 4.0, (NT,))
    growth = 3.0 ** fraction
    noise_draw = 0.6 * own_draw + 0.8 * common_draw[None, :]
    values = mode_scale * (growth * parity)[None, :] * noise_draw
    return jnp.clip(values, -18.0, 18.0).astype(jnp.bfloat16)


def draw_mode_shapes(key, part):
    key = jax.random.fold_in(key, 5)
    key_scale, key_noise = jax.random.split(key)
    elem_scale = 10.0 ** jax.random.uniform(key_scale, (NE,), minval=-0.5, maxval=0.5)
    noise_draw = jax.random.truncated_normal(key_noise, -6.0, 6.0, (M, NE))
    values = noise_draw * elem_scale[None, :] * (2.0 / math.sqrt(M))
    return jnp.clip(values, -2.5, 2.5).astype(jnp.bfloat16)


def draw_hot_owner(key, part):
    key = jax.random.fold_in(key, 7)
    busy_region = jax.random.randint(jax.random.fold_in(key, 1), (), 0, N_HA)
    blocks = N_TA * N_HA
    block_keys = jax.random.split(jax.random.fold_in(key, 2), blocks)

    def one_block(block_key):
        key_pick, key_order = jax.random.split(block_key)
        chosen = jax.random.permutation(key_pick, (N_HA - 1) * CAPB)[:HS_DEV - CAPB]
        others = (chosen // CAPB).astype(jnp.int32)
        others = others + (others >= busy_region).astype(jnp.int32)
        owners = jnp.concatenate([others, jnp.full((CAPB,), busy_region, jnp.int32)])
        shuffle = jax.random.permutation(key_order, HS_DEV)
        return owners[shuffle]
    return jax.vmap(one_block)(block_keys).reshape(blocks * HS_DEV).astype(jnp.int32)


def set_ends(entries, rng, low, top_value):
    spot = [jax.random.randint(jax.random.fold_in(rng, axis), (), 0, length) for axis, length in enumerate(entries.shape)]
    longest = entries.shape.index(max(entries.shape))
    beside = spot[:longest] + [(spot[longest] + 1) % entries.shape[longest]] + spot[longest + 1:]
    return entries.at[tuple(spot)].set(low).at[tuple(beside)].set(top_value)


def block_scale(rng, extent, pieces, least, high):
    gain, own = 1.0, jax.random.fold_in(rng, 6)
    for axis_at, blocks in pieces:
        heights = jnp.exp(jax.random.uniform(jax.random.fold_in(own, axis_at), (blocks,), jnp.float32, least / len(pieces), high / len(pieces)))
        gain = gain * jnp.repeat(heights, extent[axis_at] // blocks).reshape([-1 if axis == axis_at else 1 for axis in range(len(extent))])
    return gain


def profile(amount, total, limit, skew):
    portions = [(1 << 20) // math.isqrt(rank ** skew) + 1 for rank in range(2, amount + 1)]
    rest, counts = total - limit - (amount - 1), [1] * (amount - 1)
    while rest > 0:
        movable = [i for i in range(amount - 1) if counts[i] < limit]
        pool, left = sum([portions[i] for i in movable]), rest
        for i in movable:
            addition = min(limit - counts[i], max(1, left * portions[i] // pool), rest)
            counts[i] = counts[i] + addition
            rest = rest - addition
    return np.array([limit] + counts)


def uneven(rng, number_of, total, limit, skew):
    if number_of == 2:
        one = jax.random.randint(rng, (), max(1, total - limit), min(limit, total - 1) + 1)
        return jnp.stack([one, total - one])
    sizes = jnp.asarray(profile(number_of, total, limit, skew), jnp.int32)
    pairs = (number_of - 1) // 2
    giver, taker = sizes[1:1 + 2 * pairs:2], sizes[2:2 + 2 * pairs:2]
    margin = jnp.minimum(giver - 1, limit - taker)
    passed = jax.random.randint(jax.random.fold_in(rng, 1), (pairs,), 0, 1 << 20) % (margin + 1)
    sizes = sizes.at[1:1 + 2 * pairs:2].set(giver - passed).at[2:2 + 2 * pairs:2].set(taker + passed)
    return sizes[jax.random.permutation(jax.random.fold_in(rng, 2), number_of)]


def bell_draw(own_key, extent, spread, bound, pieces=(), kind=jnp.bfloat16):
    values = spread * jax.random.normal(own_key, extent, jnp.float32)
    if pieces:
        values = values * block_scale(own_key, extent, pieces, -0.22, 0.18)
    return jnp.clip(values, -bound, bound).astype(kind)


def setup_inputs(seed: int = 0) -> dict:
    keys = jax.random.split(jax.random.key(seed), 7)
    mode_record = draw_mode_record(jax.random.fold_in(keys[6], 71), 0)
    mode_shapes = draw_mode_shapes(jax.random.fold_in(keys[6], 71), 0)
    map_elem = set_ends(jax.random.randint(keys[2], (K_EXT, N_HA * HOT_CAP), 0, E_DEV), jax.random.fold_in(keys[2], 1), 0, E_DEV - 1).astype(jnp.int32)
    map_coef = bell_draw(keys[3], (K_EXT, N_HA * HOT_CAP), 0.5, 3.0, ((1, 32),), jnp.float32)
    hot_owner = draw_hot_owner(jax.random.fold_in(keys[6], 71), 0)
    band_bins = uneven(keys[5], NB, NT // 2, MOST_BINS, 2).astype(jnp.int32)
    return {"mode_record": mode_record, "mode_shapes": mode_shapes, "map_elem": map_elem, "map_coef": map_coef, "hot_owner": hot_owner, "band_bins": band_bins}


epsilon = 1e-06

def first_table(length):
    positions = jnp.arange(length, dtype=jnp.int32)
    angles = (positions[:, None] * positions[None, :] % length).astype(jnp.float32) * (2.0 * jnp.pi / length)
    return jnp.concatenate([jnp.cos(angles), -jnp.sin(angles)], axis=1).astype(jnp.bfloat16)

def twiddle_table(length, points):
    positions = jnp.arange(length, dtype=jnp.int32)
    angles = (positions[:, None] * positions[None, :]).astype(jnp.float32) * (2.0 * jnp.pi / points)
    return (jnp.cos(angles), jnp.sin(angles))

def second_table(length):
    positions = jnp.arange(length, dtype=jnp.int32)
    halves = jnp.arange(length // 2, dtype=jnp.int32)
    angles = (positions[:, None] * halves[None, :] % length).astype(jnp.float32) * (2.0 * jnp.pi / length)
    cos_part = jnp.cos(angles).astype(jnp.bfloat16)
    sin_part = jnp.sin(angles).astype(jnp.bfloat16)
    real_row = jnp.stack([cos_part, -sin_part], axis=1)
    imag_row = jnp.stack([sin_part, cos_part], axis=1)
    return jnp.stack([real_row, imag_row], axis=1)

def band_spectrum(series, band_index, band_bins):
    row_count = series.shape[0]
    folded = series.reshape(row_count, DFT_LEN, DFT_LEN)
    section_one = jnp.einsum('hab,ak->hbk', folded.astype(jnp.float32), first_table(DFT_LEN).astype(jnp.float32))
    turn_cos, turn_sin = twiddle_table(DFT_LEN, NT)
    real_part = section_one[:, :, :DFT_LEN]
    imag_part = section_one[:, :, DFT_LEN:]
    twiddled = jnp.stack([real_part * turn_cos + imag_part * turn_sin, imag_part * turn_cos - real_part * turn_sin], axis=2).astype(jnp.bfloat16)
    spectrum = jnp.einsum('hbrk,brsq->hqsk', twiddled.astype(jnp.float32), second_table(DFT_LEN).astype(jnp.float32))
    power_bins = (spectrum[:, :, 0, :] * spectrum[:, :, 0, :] + spectrum[:, :, 1, :] * spectrum[:, :, 1, :]).astype(jnp.bfloat16)
    power_bins = power_bins.reshape(row_count, NT // 2).astype(jnp.float32)
    band_sums = jax.ops.segment_sum(power_bins.T, band_index, num_segments=NB).T
    return band_sums / (NT * band_bins.astype(jnp.float32))[None, :]

def reference(mode_record, mode_shapes, map_elem, map_coef, hot_owner, band_bins):
    region_shapes = mode_shapes.reshape(M, N_HA, E_DEV).transpose(1, 0, 2)

    def region_rms(shapes):
        stress = jnp.dot(shapes.T, mode_record, preferred_element_type=jnp.float32)
        return jnp.sqrt(lax.optimization_barrier(jnp.sum(stress * stress, axis=1)) / NT + epsilon)
    elem_rms = lax.map(region_rms, region_shapes).reshape(NE)
    block_total = NH // HS_DEV
    owner_blocks = hot_owner.reshape(block_total, HS_DEV)
    onehot = (owner_blocks[:, :, None] == jnp.arange(N_HA, dtype=jnp.int32)[None, None, :]).astype(jnp.int32)
    before = (jnp.cumsum(onehot, axis=1).astype(jnp.int32) - onehot).astype(jnp.int32)
    slot_ranks = lax.optimization_barrier(jnp.sum(before * onehot, axis=2)).astype(jnp.int32).reshape(NH)
    block_ids = (jnp.arange(NH, dtype=jnp.int32) // HS_DEV).astype(jnp.int32)
    slot_ids = (hot_owner * HOT_CAP + block_ids * CAPB + slot_ranks).astype(jnp.int32)
    elem_ids = jnp.take(map_elem, slot_ids, axis=1)
    weights = jnp.take(map_coef, slot_ids, axis=1)
    column_ids = (hot_owner[None, :] * E_DEV + elem_ids).astype(jnp.int32)
    hot_shapes = jnp.zeros((M, NH), jnp.float32)
    for term_index in range(K_EXT):
        hot_shapes = hot_shapes + weights[term_index][None, :] * jnp.take(mode_shapes, column_ids[term_index], axis=1).astype(jnp.float32)
    bin_ids = jnp.arange(NT // 2, dtype=jnp.int32)
    band_ends = jnp.cumsum(band_bins).astype(jnp.int32)
    band_index = lax.optimization_barrier(jnp.sum((bin_ids[:, None] >= band_ends[None, :]).astype(jnp.int32), axis=1)).astype(jnp.int32)
    record_wide = mode_record.astype(jnp.float32)
    shape_blocks = hot_shapes.T.reshape(NH // HS_DEV, HS_DEV, M)

    def block_power(shapes_block):
        series = jnp.dot(shapes_block, record_wide, precision=lax.Precision.HIGHEST).astype(jnp.bfloat16)
        return band_spectrum(series, band_index, band_bins)
    band_power = lax.map(block_power, shape_blocks).reshape(NH, NB)
    return (elem_rms, band_power)
```

```python
import jax
import jax.numpy as jnp
import numpy as np
from jax import lax
from jax.experimental import pallas as pl
from jax.experimental.pallas import tpu as pltpu
from jax.sharding import PartitionSpec as P

DFT_LEN = 128
NB = 512
K_EXT = 4
HS_DEV = 32
NT = 16384
MODES = 300
E_DEV = 384
FOLD = 160
KPAD = 320
HALF = 64

epsilon = 1e-06
MESH = pl.DeviceIdType.MESH
PLANES = (0, 1, 7, 2, 6, 3, 5, 4)
PLANE_AT = {dz: i for i, dz in enumerate(PLANES)}


def tables():
    import ml_dtypes

    pos = np.arange(DFT_LEN)
    turn = np.float32(2.0 * np.pi / DFT_LEN)
    first = (pos[:, None] * pos[None, :] % DFT_LEN).astype(np.float32) * turn
    first_table = np.concatenate([np.cos(first), -np.sin(first)], axis=0)
    fine = (pos[:, None] * pos[None, :]).astype(np.float32) * np.float32(2.0 * np.pi / NT)
    twiddle = []
    for half in range(2):
        part = fine[:, half * HALF : (half + 1) * HALF]
        part = np.concatenate([part, part], axis=1)
        twiddle += [np.cos(part), np.sin(part)]
    second = np.zeros((4, 2, HALF, 2, 2, HALF), np.float32)
    for half in range(2):
        angles = first[half * HALF : (half + 1) * HALF, :HALF]
        c, s = np.cos(angles), np.sin(angles)
        for hh in range(2):
            second[2 * half, hh, :, 0, hh] = c
            second[2 * half, hh, :, 1, hh] = -s
            second[2 * half + 1, hh, :, 0, hh] = s
            second[2 * half + 1, hh, :, 1, hh] = c
    return (
        first_table.astype(ml_dtypes.bfloat16),
        np.stack(twiddle).astype(np.float32),
        second.reshape(512, 256).astype(ml_dtypes.bfloat16),
    )


def kernel(
    rec_ref, shapes_ref, elem_ref, coef_ref, owner_ref, bins_ref, first_ref, turn_ref, second_ref,
    band_ref, energy_ref,
    pad_rec, pad_shapes, shapes_out, shapes_in, shapes_t,
    c_rows, c_out, c_in, c_flat, hot_mine, hot_in,
    gathered, wide, folded, sending, arrived,
    member, power, power_rows, table, e_acc, e_mine, e_in, e_sum, e_all,
    shp_ss, shp_rs, c_ss, c_rs, hot_ss, hot_rs, g_ss, g_rs, s_ss, s_rs, e1_ss, e1_rs, e2_ss, e2_rs,
):
    f32, bf16, i32 = jnp.float32, jnp.bfloat16, jnp.int32
    z = lax.axis_index("ta")
    ha = lax.axis_index("ha")
    core = lax.rem(ha, 2)
    x = lax.div(ha, 8)
    y = lax.rem(lax.div(ha, 2), 4)
    u = jnp.where(core == 0, x, y)
    v = jnp.where(core == 0, y, x)
    z_half, z_odd = lax.div(z, 2), lax.rem(z, 2)

    def at(px, py, pz, pc):
        return (pz, (px * 4 + py) * 2 + pc)

    def line(plane_core, pu, pv, pz, pc):
        return at(
            jnp.where(plane_core == 0, pu, pv), jnp.where(plane_core == 0, pv, pu), pz, pc
        )

    def send(src, dst, ss, rs, device):
        copy = pltpu.make_async_remote_copy(
            src_ref=src, dst_ref=dst, send_sem=ss, recv_sem=rs, device_id=device, device_id_type=MESH
        )
        copy.start()
        return copy

    def wait(ref, sem):
        pltpu.make_async_copy(ref, ref, sem).wait()

    barrier = pltpu.get_barrier_semaphore()

    def greet_plane(o, _):
        pl.semaphore_signal(
            barrier, inc=1, device_id=(z, lax.rem(ha + o, 32)), device_id_type=MESH
        )
        return 0

    def greet_line(o, _):
        pl.semaphore_signal(barrier, inc=1, device_id=(lax.rem(z + o, 8), ha), device_id_type=MESH)
        return 0

    lax.fori_loop(1, 32, greet_plane, 0)
    lax.fori_loop(1, 8, greet_line, 0)

    lane128 = lax.broadcasted_iota(i32, (1, 128), 1)
    left = lane128 < HALF

    def swap(tile):
        return pltpu.roll(tile, HALF, 1)

    pad_rec[...] = jnp.zeros_like(pad_rec)
    pad_rec[0:HALF, 0:MODES] = rec_ref[...].astype(f32)
    turned = pad_rec[...].T
    gathered[0] = (turned[0:FOLD] + swap(turned[FOLD : 2 * FOLD])).astype(bf16)

    shapes_out[MODES - 12 : 304, :] = jnp.zeros((16, E_DEV), bf16)
    shapes_out[0:MODES, :] = shapes_ref[...]
    slots = pl.ds(pl.multiple_of(z_half * 128, 128), 128)
    elems = elem_ref[:, slots]
    coefs = coef_ref[:, slots]
    elem_ids = lax.broadcasted_iota(i32, (E_DEV, 128), 0)
    hot = jnp.zeros((304, 128), f32)
    for k in range(K_EXT):
        pick = (elem_ids == elems[k : k + 1, :]).astype(f32).astype(bf16)
        hot = hot + coefs[k : k + 1, :] * jnp.dot(
            shapes_out[...], pick, preferred_element_type=f32
        )
    c_rows[...] = jnp.concatenate([hot, jnp.zeros((80, 128), f32)], axis=0).T

    def spread(i, _):
        c_out[i] = c_rows[pl.ds(z_odd * HALF + i, 1), :]
        return 0

    lax.fori_loop(0, 64, spread, 0)

    col = lax.broadcasted_iota(i32, (128, 128), 1)
    row = lax.broadcasted_iota(i32, (128, 128), 0)
    source, place, dv = lax.div(col, 32), lax.div(lax.rem(col, 32), 4), lax.rem(col, 4)
    dz = jnp.zeros_like(col)
    for i, value in enumerate(PLANES):
        dz = jnp.where(place == i, value, dz)
    zz = lax.rem(z + dz, 8)
    a_even = 16 * zz + 4 * lax.rem(x + source, 4) + lax.rem(y + dv, 4)
    a_odd = 16 * zz + 4 * lax.rem(x + dv, 4) + lax.rem(y + source, 4)
    for half, a_of in enumerate((a_even, a_odd)):
        order = (row == a_of).astype(f32).astype(bf16)
        table[half] = jnp.dot(first_ref[...], order, preferred_element_type=f32).astype(bf16)

    pl.semaphore_wait(barrier, 38)

    copies = []
    g_count = [0]

    def g_send(q, j, rows, dq, dj, device):
        n = g_count[0]
        g_count[0] += 1
        copies.append(
            send(
                gathered.at[q * 4 + j], gathered.at[dq * 4 + dj], g_ss.at[n],
                g_rs.at[dq * 4 + dj], device,
            )
        )

    up, down = lax.rem(z + 1, 8), lax.rem(z + 7, 8)

    def z_send(k, j, go_up):
        here = (8 - k) % 8 if go_up else k
        there = (8 - k - 1) % 8 if go_up else k + 1
        g_send(
            PLANE_AT[here], j, None, PLANE_AT[there], j,
            line(core, u, v, up if go_up else down, core),
        )

    def g_wait(q, j):
        wait(gathered.at[q * 4 + j], g_rs.at[q * 4 + j])

    for j in (1, 3, 2):
        g_send(0, 0, None, 0, j, line(core, u, lax.rem(v + 4 - j, 4), z, core))
    z_send(0, 0, True)
    z_send(0, 0, False)

    def c_send(o, _):
        to = lax.rem(ha + o, 32)
        pltpu.make_async_remote_copy(
            src_ref=c_out.at[pl.ds(2 * to, 2)], dst_ref=c_in.at[pl.ds(2 * (32 - o), 2)],
            send_sem=c_ss, recv_sem=c_rs, device_id=(z, to), device_id_type=MESH,
        ).start()
        return 0

    lax.fori_loop(1, 32, c_send, 0)
    c_in[0] = c_out[2 * ha]
    c_in[1] = c_out[2 * ha + 1]

    owns = core == z_odd
    shp_to = [
        line(0, lax.rem(x + 4 - z_half, 4), y, z, 0),
        line(1, lax.rem(y + 4 - z_half, 4), x, z, 1),
    ]

    def shape_copies(act):
        for cc in range(2):
            own_work = jnp.logical_and(z_half == 0, core == cc)

            @pl.when(jnp.logical_and(owns, jnp.logical_not(own_work)))
            def _():
                act(
                    pltpu.make_async_remote_copy(
                        src_ref=shapes_out, dst_ref=shapes_in, send_sem=shp_ss.at[cc],
                        recv_sem=shp_rs, device_id=shp_to[cc], device_id_type=MESH,
                    )
                )

    shape_copies(lambda copy: copy.start())
    local_shapes = jnp.logical_and(owns, z_half == 0)

    @pl.when(local_shapes)
    def _():
        shapes_in[...] = shapes_out[...]

    for j in (1, 3, 2):
        g_wait(0, j)
        z_send(0, j, True)
        z_send(0, j, False)

    bins = bins_ref[...].astype(f32)
    before = (
        lax.broadcasted_iota(i32, (NB, NB), 0) < lax.broadcasted_iota(i32, (NB, NB), 1)
    ).astype(f32).astype(bf16)
    starts = jnp.dot(
        jnp.broadcast_to(bins, (8, NB)).astype(bf16), before, preferred_element_type=f32
    )[0:1]
    starts_i = starts.astype(i32)
    ends_i = (starts + bins).astype(i32)

    def member_block(i, _):
        rows = lax.broadcasted_iota(i32, (256, 1), 0)
        bin_ids = i * 4 + lax.div(rows, HALF) + DFT_LEN * lax.rem(rows, HALF)
        inside = jnp.logical_and(bin_ids >= starts_i, bin_ids < ends_i)
        member[pl.ds(pl.multiple_of(i * 256, 256), 256), :] = inside.astype(f32).astype(bf16)
        return 0

    lax.fori_loop(0, 16, member_block, 0)

    def step(k):
        for j in (0, 1, 3, 2):
            for go_up in (True, False):
                here = (8 - k) % 8 if go_up else k
                g_wait(PLANE_AT[here], j)
                if k < 3 or (j in (0, 1)) == go_up:
                    z_send(k, j, go_up)

    step(1)

    wait(c_in.at[pl.ds(2, 62)], c_rs)

    def flatten(i, _):
        c_flat[pl.ds(i, 1), :] = c_in[i]
        return 0

    lax.fori_loop(0, 64, flatten, 0)
    owner_row = owner_ref[...]
    r32 = lax.broadcasted_iota(i32, (32, 32), 0)
    c32 = lax.broadcasted_iota(i32, (32, 32), 1)
    owners = jnp.broadcast_to(owner_row, (32, 32))
    owner_col = jnp.sum(jnp.where(r32 == c32, owners, 0), axis=1, keepdims=True)
    rank = jnp.sum(
        jnp.logical_and(owners == owner_col, c32 < r32).astype(i32), axis=1, keepdims=True
    )
    slot = lax.broadcasted_iota(i32, (32, 64), 1)
    region = lax.rem(ha + lax.div(slot, 2), 32)
    chosen = jnp.logical_and(region == owner_col, lax.rem(slot, 2) == rank)
    chosen = chosen.astype(f32).astype(bf16)
    flat = c_flat[...]
    high = flat.astype(bf16)
    low = (flat - high.astype(f32)).astype(bf16)
    high = jnp.dot(chosen, high, preferred_element_type=f32)
    low = jnp.dot(chosen, low, preferred_element_type=f32)
    hot_mine[...] = jnp.concatenate(
        [high[:, 0:256], high[:, 256:384] + swap(low[:, 256:384]), low[:, 0:256]], axis=1
    ).astype(bf16)
    hot_in[core] = hot_mine[...]
    for du in range(1, 4):
        for cc in range(2):
            here_u, here_v = (x, y) if cc == 0 else (y, x)
            copies.append(
                send(
                    hot_mine, hot_in.at[du * 2 + core], hot_ss.at[du * 2 + cc],
                    hot_rs.at[du * 2 + core], line(cc, lax.rem(here_u + 4 - du, 4), here_v, z, cc),
                )
            )
    copies.append(
        send(hot_mine, hot_in.at[core], hot_ss.at[0], hot_rs.at[core], at(x, y, z, 1 - core))
    )

    lax.fori_loop(16, 32, member_block, 0)
    step(2)

    @pl.when(jnp.logical_not(local_shapes))
    def _():
        wait(shapes_in, shp_rs)

    pad_shapes[0:304, :] = shapes_in[...].astype(f32)
    pad_shapes[304:384, :] = jnp.zeros((80, E_DEV), f32)
    shapes_t[...] = pad_shapes[...].T.astype(bf16)
    e_acc[...] = jnp.zeros_like(e_acc)

    def unfold(q):
        parts = []
        for pair in range(2):
            even = gathered[q * 4 + 2 * pair].astype(f32)
            odd = gathered[q * 4 + 2 * pair + 1].astype(f32)
            parts.append(
                (
                    jnp.where(left, even, swap(odd)).astype(bf16),
                    jnp.where(left, swap(even), odd).astype(bf16),
                )
            )
        first = jnp.concatenate([parts[0][0], parts[1][0]], axis=1)
        last = jnp.concatenate([parts[0][1], parts[1][1]], axis=1)
        wide[0:160, :] = first
        wide[160:320, :] = last
        wide[320:384, :] = last[96:160]
        wide[384:544, :] = first
        wide[544:640, :] = last[0:96]

    def energies():
        stress = jnp.dot(shapes_t[...], wide[0:384, :], preferred_element_type=f32)
        squares = stress * stress
        e_acc[...] += squares[:, 0:128] + squares[:, 128:256]

    def series(q):
        out = jnp.dot(
            hot_in[...].reshape(256, 640), wide[...], preferred_element_type=f32
        ).reshape(8, 2, 16, 256)
        for pair in range(2):
            lanes = slice(pair * 128, pair * 128 + 128)
            top = out[:, 0, :, lanes].reshape(128, 128)
            low_half = out[:, 1, :, lanes].reshape(128, 128)
            for n, tile in enumerate(
                (
                    jnp.where(left, top, swap(low_half)),
                    jnp.where(left, swap(top), low_half),
                )
            ):
                folded[pl.ds((q % 4) * 4 + pair * 2 + n, 128, stride=16), :] = tile

    def s_send(piece):
        sending[piece] = folded[...].astype(bf16).reshape(8, 16, 16, 128)
        arrived[core, 0, piece] = sending[piece, core]
        for du in range(1, 4):
            for cc in range(2):
                n = du * 2 + cc
                copies.append(
                    send(
                        sending.at[piece, n], arrived.at[core, (4 - du) % 4, piece],
                        s_ss.at[piece, n], s_rs.at[core, (4 - du) % 4, piece],
                        line(core, lax.rem(u + du, 4), v, z, cc),
                    )
                )
        copies.append(
            send(
                sending.at[piece, 1 - core], arrived.at[core, 0, piece], s_ss.at[piece, 0],
                s_rs.at[core, 0, piece], at(x, y, z, 1 - core),
            )
        )

    for du in range(1, 4):
        for cc in range(2):
            wait(hot_in.at[du * 2 + cc], hot_rs.at[du * 2 + cc])
    wait(hot_in.at[1 - core], hot_rs.at[1 - core])

    for q in range(4):
        unfold(q)
        series(q)
        energies()
    s_send(0)
    step(3)
    for q in range(4, 7):
        unfold(q)
        series(q)
        energies()
    for j in range(4):
        g_wait(7, j)
    unfold(7)
    series(7)
    s_send(1)
    energies()

    e_mine[0] = jnp.sum(e_acc[...].T, axis=0, keepdims=True)
    e_local = jnp.logical_and(z_half == 0, core == z_odd)
    e_to = line(core, lax.rem(u + z_half, 4), v, z, z_odd)

    def e_first(act):
        @pl.when(jnp.logical_not(e_local))
        def _():
            act(
                pltpu.make_async_remote_copy(
                    src_ref=e_mine, dst_ref=e_in.at[pl.ds(core, 1)], send_sem=e1_ss,
                    recv_sem=e1_rs.at[core], device_id=e_to, device_id_type=MESH,
                )
            )

    e_first(lambda copy: copy.start())

    @pl.when(e_local)
    def _():
        e_in[core] = e_mine[0]

    def e_second(act):
        @pl.when(owns)
        def _():
            def one(o, _):
                act(
                    pltpu.make_async_remote_copy(
                        src_ref=e_sum, dst_ref=e_all.at[pl.ds(z_half, 1)], send_sem=e2_ss.at[o],
                        recv_sem=e2_rs.at[z_half], device_id=(lax.rem(z + o, 8), ha),
                        device_id_type=MESH,
                    )
                )
                return 0

            lax.fori_loop(1, 8, one, 0)

    @pl.when(owns)
    def _():
        for cc in range(2):

            @pl.when(jnp.logical_not(jnp.logical_and(z_half == 0, core == cc)))
            def _():
                wait(e_in.at[pl.ds(cc, 1)], e1_rs.at[cc])

        e_sum[0] = e_in[0] + e_in[1]
        e_all[z_half] = e_sum[0]

    e_second(lambda copy: copy.start())

    for piece in range(2):
        for half in range(2):
            for du in range(1, 4):
                wait(arrived.at[half, du, piece], s_rs.at[half, du, piece])
        wait(arrived.at[1 - core, 0, piece], s_rs.at[1 - core, 0, piece])

    def spectrum(pp, _):
        ones = []
        for half in range(2):
            tiles = []
            for n in range(2):
                tiles.append(
                    jnp.concatenate(
                        [
                            arrived[half, i, piece, 2 * pp + n]
                            for i in range(4)
                            for piece in range(2)
                        ],
                        axis=0,
                    )
                )
            one = jnp.dot(
                table[half], jnp.concatenate(tiles, axis=1), preferred_element_type=f32
            )
            ones.append(one)
        for n in range(2):
            lanes = slice(n * 128, n * 128 + 128)
            blocks = []
            for half in range(2):
                real, imag = ones[half][0:128, lanes], ones[half][128:256, lanes]
                c, s = turn_ref[2 * half], turn_ref[2 * half + 1]
                blocks += [(real * c + imag * s).astype(bf16), (imag * c - real * s).astype(bf16)]
            out = jnp.dot(
                jnp.concatenate(blocks, axis=1), second_ref[...], preferred_element_type=f32
            )
            real, imag = out[:, 0:128], out[:, 128:256]
            power[pl.ds(2 * pp + n, 128, stride=16), :] = real * real + imag * imag
        return 0

    lax.fori_loop(0, 8, spectrum, 0)

    for kb in range(32):
        tiles = []
        for pair in range(2):
            base = (kb * 4 + pair * 2) * 16
            even, odd = power[base : base + 16, :], power[base + 16 : base + 32, :]
            tiles.append(
                jnp.concatenate(
                    [jnp.where(left, even, swap(odd)), jnp.where(left, swap(even), odd)], axis=0
                )
            )
        power_rows[:, kb * 256 : kb * 256 + 256] = jnp.concatenate(tiles, axis=1).astype(bf16)
    band_ref[...] = jnp.dot(power_rows[...], member[...], preferred_element_type=f32)

    for i in range(4):

        @pl.when(jnp.logical_not(jnp.logical_and(owns, z_half == i)))
        def _():
            wait(e_all.at[pl.ds(i, 1)], e2_rs.at[i])

    energy_ref[...] = (e_all[0] + e_all[1]) + (e_all[2] + e_all[3])

    for copy in copies:
        copy.wait_send()
    wait(c_out.at[pl.ds(2, 62)], c_ss)
    shape_copies(lambda copy: copy.wait_send())
    e_first(lambda copy: copy.wait_send())
    e_second(lambda copy: copy.wait_send())


def shards(mode_record, mode_shapes, map_elem, map_coef, hot_owner, band_bins):
    f32, bf16 = jnp.float32, jnp.bfloat16
    first, turn, second = tables()
    vmem, dma = pltpu.VMEM, pltpu.SemaphoreType.DMA
    scratch = [
        vmem((128, 384), f32),
        vmem((384, 384), f32),
        vmem((304, 384), bf16),
        vmem((304, 384), bf16),
        vmem((384, 384), bf16),
        vmem((128, 384), f32),
        vmem((64, 1, 384), f32),
        vmem((64, 1, 384), f32),
        vmem((64, 384), f32),
        vmem((32, 640), bf16),
        vmem((8, 32, 640), bf16),
        vmem((32, FOLD, 128), bf16),
        vmem((640, 256), bf16),
        vmem((2048, 128), f32),
        vmem((2, 8, 16, 16, 128), bf16),
        vmem((2, 4, 2, 16, 16, 128), bf16),
        vmem((NT // 2, NB), bf16),
        vmem((2048, 128), f32),
        vmem((32, NT // 2), bf16),
        vmem((2, 256, 128), bf16),
        vmem((384, 128), f32),
        vmem((1, 1, 384), f32),
        vmem((2, 1, 384), f32),
        vmem((1, 1, 384), f32),
        vmem((4, 1, 384), f32),
        dma((2,)), dma, dma, dma, dma((8,)), dma((8,)), dma((31,)), dma((32,)),
        dma((2, 8)), dma((2, 4, 2)), dma, dma((2,)), dma((8,)), dma((4,)),
    ]
    whole = pl.BlockSpec(memory_space=pltpu.VMEM)
    sums, energy = pl.pallas_call(
        kernel,
        out_shape=(
            jax.ShapeDtypeStruct((HS_DEV, NB), f32),
            jax.ShapeDtypeStruct((1, E_DEV), f32),
        ),
        in_specs=[whole] * 9,
        out_specs=(whole, whole),
        scratch_shapes=scratch,
        compiler_params=pltpu.CompilerParams(
            collective_id=0, has_side_effects=True, vmem_limit_bytes=48 * 2**20
        ),
        name="whipping",
    )(
        mode_record.T, mode_shapes, map_elem, map_coef, hot_owner.reshape(1, HS_DEV),
        band_bins.reshape(1, NB), jnp.asarray(first), jnp.asarray(turn), jnp.asarray(second),
    )
    elem_rms = jnp.sqrt(energy.reshape(E_DEV) / NT + epsilon)
    band_power = sums / (NT * band_bins.astype(f32))[None, :]
    return (elem_rms, band_power)


def solution(mesh):
    in_specs = (
        P(None, ("ta", "ha")),
        P(None, "ha"),
        P(None, "ha"),
        P(None, "ha"),
        P(("ta", "ha")),
        P(),
    )
    out_specs = (P("ha"), P(("ta", "ha"), None))
    return jax.shard_map(shards, mesh=mesh, in_specs=in_specs, out_specs=out_specs, check_vma=False)
```

```python
import jax
import jax.numpy as jnp
import numpy as np
from jax import lax
from jax.experimental import pallas as pl
from jax.experimental.pallas import tpu as pltpu
from jax.sharding import PartitionSpec as P

DFT_LEN = 128
NB = 512
K_EXT = 4
HS_DEV = 32
NT = 16384
MODES = 300
E_DEV = 384
FOLD = 160
KPAD = 320
HALF = 64

epsilon = 1e-06
MESH = pl.DeviceIdType.MESH
PLANES = (0, 1, 7, 2, 6, 3, 5, 4)
PLANE_AT = {dz: i for i, dz in enumerate(PLANES)}


def tables():
    import ml_dtypes

    pos = np.arange(DFT_LEN)
    turn = np.float32(2.0 * np.pi / DFT_LEN)
    first = (pos[:, None] * pos[None, :] % DFT_LEN).astype(np.float32) * turn
    first_table = np.concatenate([np.cos(first), -np.sin(first)], axis=0)
    fine = (pos[:, None] * pos[None, :]).astype(np.float32) * np.float32(2.0 * np.pi / NT)
    twiddle = []
    for half in range(2):
        part = fine[:, half * HALF : (half + 1) * HALF]
        part = np.concatenate([part, part], axis=1)
        twiddle += [np.cos(part), np.sin(part)]
    second = np.zeros((4, 2, HALF, 2, 2, HALF), np.float32)
    for half in range(2):
        angles = first[half * HALF : (half + 1) * HALF, :HALF]
        c, s = np.cos(angles), np.sin(angles)
        for hh in range(2):
            second[2 * half, hh, :, 0, hh] = c
            second[2 * half, hh, :, 1, hh] = -s
            second[2 * half + 1, hh, :, 0, hh] = s
            second[2 * half + 1, hh, :, 1, hh] = c
    return (
        first_table.astype(ml_dtypes.bfloat16),
        np.stack(twiddle).astype(np.float32),
        second.reshape(512, 256).astype(ml_dtypes.bfloat16).astype(np.float32),
    )


def kernel(
    rec_hbm, shapes_hbm, elem_hbm, coef_hbm, owner_hbm, bins_hbm, first_hbm, turn_hbm, second_hbm,
    band_ref, energy_ref,
    rec_ref, shapes_ref, elem_ref, coef_ref, owner_ref, bins_ref, first_ref, turn_ref, second_ref,
    pad_rec, pad_shapes, shapes_out, shapes_in, shapes_t,
    c_rows, c_out, c_in, c_flat, hot_mine, hot_in,
    gathered, wide, folded, sending, arrived,
    member, twiddled, power, table, e_acc, e_mine, e_in, e_sum, e_all,
    shp_ss, shp_rs, c_ss, c_rs, hot_ss, hot_rs, g_ss, g_rs, z_ss, far_rs, s_ss, s_rs, e1_ss, e1_rs, e2_ss, e2_rs,
    in_sem,
):
    f32, bf16, i32 = jnp.float32, jnp.bfloat16, jnp.int32
    z = lax.axis_index("ta")
    ha = lax.axis_index("ha")
    core = lax.rem(ha, 2)
    x = lax.div(ha, 8)
    y = lax.rem(lax.div(ha, 2), 4)
    u = jnp.where(core == 0, x, y)
    v = jnp.where(core == 0, y, x)
    z_half, z_odd = lax.div(z, 2), lax.rem(z, 2)

    def at(px, py, pz, pc):
        return (pz, (px * 4 + py) * 2 + pc)

    def line(plane_core, pu, pv, pz, pc):
        return at(
            jnp.where(plane_core == 0, pu, pv), jnp.where(plane_core == 0, pv, pu), pz, pc
        )

    def send(src, dst, ss, rs, device):
        copy = pltpu.make_async_remote_copy(
            src_ref=src, dst_ref=dst, send_sem=ss, recv_sem=rs, device_id=device, device_id_type=MESH
        )
        copy.start()
        return copy

    def wait(ref, sem):
        pltpu.make_async_copy(ref, ref, sem).wait()

    fetches = [
        pltpu.make_async_copy(src, dst, in_sem.at[n])
        for n, (src, dst) in enumerate(
            (
                (rec_hbm, rec_ref), (shapes_hbm, shapes_ref), (elem_hbm, elem_ref),
                (coef_hbm, coef_ref), (first_hbm, first_ref), (bins_hbm, bins_ref),
                (owner_hbm, owner_ref), (second_hbm, second_ref), (turn_hbm, turn_ref),
            )
        )
    ]
    for fetch in fetches:
        fetch.start()

    barrier = pltpu.get_barrier_semaphore()

    def greet_plane(o, _):
        pl.semaphore_signal(
            barrier, inc=1, device_id=(z, lax.rem(ha + o, 32)), device_id_type=MESH
        )
        return 0

    def greet_line(o, _):
        pl.semaphore_signal(barrier, inc=1, device_id=(lax.rem(z + o, 8), ha), device_id_type=MESH)
        return 0

    lax.fori_loop(1, 32, greet_plane, 0)
    lax.fori_loop(1, 8, greet_line, 0)

    lane128 = lax.broadcasted_iota(i32, (1, 128), 1)
    left = lane128 < HALF

    def swap(tile):
        return pltpu.roll(tile, HALF, 1)

    pad_rec[...] = jnp.zeros_like(pad_rec)
    fetches[0].wait()
    pad_rec[0:HALF, 0:MODES] = rec_ref[...].astype(f32)
    turned = pad_rec[...].T
    gathered[0] = (turned[0:FOLD] + swap(turned[FOLD : 2 * FOLD])).astype(bf16)

    shapes_out[MODES - 12 : 304, :] = jnp.zeros((16, E_DEV), bf16)
    for fetch in fetches[1:4]:
        fetch.wait()
    shapes_out[0:MODES, :] = shapes_ref[...]
    pl.semaphore_wait(barrier, 38)

    copies = []

    def g_send(n, q, dq, j, device):
        copies.append(
            send(gathered.at[q * 4], gathered.at[dq * 4 + j], g_ss.at[n], g_rs.at[dq * 4 + j], device)
        )

    def g_wait(q, j):
        wait(gathered.at[q * 4 + j], g_rs.at[q * 4 + j])

    def v_send(q):
        for j in (1, 3, 2):
            g_send(3 * q + j - 1, q, q, j, line(core, u, lax.rem(v + 4 - j, 4), z, core))

    def z_send(n, q, dq, dz, rows=None):
        src, dst = gathered.at[q * 4], gathered.at[dq * 4]
        rs = g_rs.at[dq * 4]
        if rows is not None:
            src, dst = src.at[pl.ds(rows, FOLD // 2)], dst.at[pl.ds(rows, FOLD // 2)]
            rs = far_rs.at[rows // (FOLD // 2)]
        copies.append(send(src, dst, z_ss.at[n], rs, at(x, y, lax.rem(z + 8 + dz, 8), core)))

    for n, dz in enumerate((1, 7, 2, 6)):
        z_send(n, 0, PLANE_AT[dz], -dz)
    v_send(0)

    slots = pl.ds(pl.multiple_of(z_half * 128, 128), 128)
    elems = elem_ref[:, slots]
    coefs = coef_ref[:, slots]
    elem_ids = lax.broadcasted_iota(i32, (E_DEV, 128), 0)
    hot = jnp.zeros((304, 128), f32)
    for k in range(K_EXT):
        pick = (elem_ids == elems[k : k + 1, :]).astype(f32).astype(bf16)
        hot = hot + coefs[k : k + 1, :] * jnp.dot(
            shapes_out[...], pick, preferred_element_type=f32
        )
    c_rows[...] = jnp.concatenate([hot, jnp.zeros((80, 128), f32)], axis=0).T

    def spread(i, _):
        c_out[i] = c_rows[pl.ds(z_odd * HALF + i, 1), :]
        return 0

    lax.fori_loop(0, 64, spread, 0)

    def c_send(o, _):
        to = lax.rem(ha + o, 32)
        pltpu.make_async_remote_copy(
            src_ref=c_out.at[pl.ds(2 * to, 2)], dst_ref=c_in.at[pl.ds(2 * (32 - o), 2)],
            send_sem=c_ss, recv_sem=c_rs, device_id=(z, to), device_id_type=MESH,
        ).start()
        return 0

    lax.fori_loop(1, 32, c_send, 0)
    c_in[0] = c_out[2 * ha]
    c_in[1] = c_out[2 * ha + 1]

    owns = core == z_odd
    shp_to = [
        line(0, lax.rem(x + 4 - z_half, 4), y, z, 0),
        line(1, lax.rem(y + 4 - z_half, 4), x, z, 1),
    ]

    def shape_copies(act):
        for cc in range(2):
            own_work = jnp.logical_and(z_half == 0, core == cc)

            @pl.when(jnp.logical_and(owns, jnp.logical_not(own_work)))
            def _():
                act(
                    pltpu.make_async_remote_copy(
                        src_ref=shapes_out, dst_ref=shapes_in, send_sem=shp_ss.at[cc],
                        recv_sem=shp_rs, device_id=shp_to[cc], device_id_type=MESH,
                    )
                )

    shape_copies(lambda copy: copy.start())
    local_shapes = jnp.logical_and(owns, z_half == 0)

    @pl.when(local_shapes)
    def _():
        shapes_in[...] = shapes_out[...]

    for q in (PLANE_AT[1], PLANE_AT[7]):
        g_wait(q, 0)
        v_send(q)

    col = lax.broadcasted_iota(i32, (128, 128), 1)
    row = lax.broadcasted_iota(i32, (128, 128), 0)
    source, place, dv = lax.div(col, 32), lax.div(lax.rem(col, 32), 4), lax.rem(col, 4)
    dz = jnp.zeros_like(col)
    for i, value in enumerate(PLANES):
        dz = jnp.where(place == i, value, dz)
    zz = lax.rem(z + dz, 8)
    a_even = 16 * zz + 4 * lax.rem(x + source, 4) + lax.rem(y + dv, 4)
    a_odd = 16 * zz + 4 * lax.rem(x + dv, 4) + lax.rem(y + source, 4)
    fetches[4].wait()
    for half, a_of in enumerate((a_even, a_odd)):
        order = (row == a_of).astype(f32).astype(bf16)
        table[half] = jnp.dot(first_ref[...], order, preferred_element_type=f32).astype(bf16)

    for fetch in fetches[5:]:
        fetch.wait()
    bins = bins_ref[...].astype(f32)
    before = (
        lax.broadcasted_iota(i32, (NB, NB), 0) < lax.broadcasted_iota(i32, (NB, NB), 1)
    ).astype(f32).astype(bf16)
    starts = jnp.dot(
        jnp.broadcast_to(bins, (8, NB)).astype(bf16), before, preferred_element_type=f32
    )[0:1]
    starts_i = starts.astype(i32)
    ends_i = (starts + bins).astype(i32)

    def member_block(i, _):
        rows = lax.broadcasted_iota(i32, (256, 1), 0)
        bin_ids = i * 4 + lax.div(rows, HALF) + DFT_LEN * lax.rem(rows, HALF)
        inside = jnp.logical_and(bin_ids >= starts_i, bin_ids < ends_i)
        member[pl.ds(pl.multiple_of(i * 256, 256), 256), :] = inside.astype(f32).astype(bf16)
        return 0

    for n, (dz, step) in enumerate(((2, -1), (6, 1))):
        q = PLANE_AT[dz]
        g_wait(q, 0)
        z_send(4 + 2 * n, q, PLANE_AT[(dz - step) % 8], step)
        z_send(5 + 2 * n, q, PLANE_AT[4], 2 * step, n * (FOLD // 2))
        v_send(q)

    wait(c_in.at[pl.ds(2, 62)], c_rs)

    def flatten(i, _):
        c_flat[pl.ds(i, 1), :] = c_in[i]
        return 0

    lax.fori_loop(0, 64, flatten, 0)
    owner_row = owner_ref[...]
    r32 = lax.broadcasted_iota(i32, (32, 32), 0)
    c32 = lax.broadcasted_iota(i32, (32, 32), 1)
    owners = jnp.broadcast_to(owner_row, (32, 32))
    owner_col = jnp.sum(jnp.where(r32 == c32, owners, 0), axis=1, keepdims=True)
    rank = jnp.sum(
        jnp.logical_and(owners == owner_col, c32 < r32).astype(i32), axis=1, keepdims=True
    )
    slot = lax.broadcasted_iota(i32, (32, 64), 1)
    region = lax.rem(ha + lax.div(slot, 2), 32)
    chosen = jnp.logical_and(region == owner_col, lax.rem(slot, 2) == rank)
    chosen = chosen.astype(f32).astype(bf16)
    flat = c_flat[...]
    high = flat.astype(bf16)
    low = (flat - high.astype(f32)).astype(bf16)
    high = jnp.dot(chosen, high, preferred_element_type=f32)
    low = jnp.dot(chosen, low, preferred_element_type=f32)
    hot_mine[...] = jnp.concatenate(
        [high[:, 0:256], high[:, 256:384] + swap(low[:, 256:384]), low[:, 0:256]], axis=1
    ).astype(bf16)
    hot_in[core] = hot_mine[...]
    for du in range(1, 4):
        for cc in range(2):
            here_u, here_v = (x, y) if cc == 0 else (y, x)
            copies.append(
                send(
                    hot_mine, hot_in.at[du * 2 + core], hot_ss.at[du * 2 + cc],
                    hot_rs.at[du * 2 + core], line(cc, lax.rem(here_u + 4 - du, 4), here_v, z, cc),
                )
            )
    copies.append(
        send(hot_mine, hot_in.at[core], hot_ss.at[0], hot_rs.at[core], at(x, y, z, 1 - core))
    )

    for q in (PLANE_AT[3], PLANE_AT[5]):
        g_wait(q, 0)
        v_send(q)
    for n in range(2):
        wait(gathered.at[PLANE_AT[4] * 4, pl.ds(n * (FOLD // 2), FOLD // 2)], far_rs.at[n])
    v_send(PLANE_AT[4])

    lax.fori_loop(0, 32, member_block, 0)

    @pl.when(jnp.logical_not(local_shapes))
    def _():
        wait(shapes_in, shp_rs)

    pad_shapes[0:304, :] = shapes_in[...].astype(f32)
    pad_shapes[304:384, :] = jnp.zeros((80, E_DEV), f32)
    shapes_t[...] = pad_shapes[...].T.astype(bf16)
    e_acc[...] = jnp.zeros_like(e_acc)

    def unfold(q):
        parts = []
        for pair in range(2):
            even = gathered[q * 4 + 2 * pair].astype(f32)
            odd = gathered[q * 4 + 2 * pair + 1].astype(f32)
            parts.append(
                (
                    jnp.where(left, even, swap(odd)).astype(bf16),
                    jnp.where(left, swap(even), odd).astype(bf16),
                )
            )
        first = jnp.concatenate([parts[0][0], parts[1][0]], axis=1)
        last = jnp.concatenate([parts[0][1], parts[1][1]], axis=1)
        wide[q, 0:160, :] = first
        wide[q, 160:320, :] = last
        wide[q, 320:384, :] = last[96:160]
        wide[q, 384:544, :] = first
        wide[q, 544:640, :] = last[0:96]

    def energies(q):
        stress = jnp.dot(shapes_t[...], wide[q, 0:384, :], preferred_element_type=f32)
        squares = stress * stress
        e_acc[...] += squares[:, 0:128] + squares[:, 128:256]

    def series(q):
        out = jnp.dot(
            hot_in[...].reshape(256, 640), wide[q], preferred_element_type=f32
        ).reshape(8, 2, 16, 256)
        for pair in range(2):
            lanes = slice(pair * 128, pair * 128 + 128)
            top = out[:, 0, :, lanes].reshape(128, 128)
            low_half = out[:, 1, :, lanes].reshape(128, 128)
            for n, tile in enumerate(
                (
                    jnp.where(left, top, swap(low_half)),
                    jnp.where(left, swap(top), low_half),
                )
            ):
                folded[pl.ds((q % 4) * 4 + pair * 2 + n, 128, stride=16), :] = tile

    def s_send(piece):
        sending[piece] = folded[...].astype(bf16).reshape(8, 16, 16, 128)
        arrived[core, 0, piece] = sending[piece, core]
        for du in range(1, 4):
            for cc in range(2):
                n = du * 2 + cc
                copies.append(
                    send(
                        sending.at[piece, n], arrived.at[core, (4 - du) % 4, piece],
                        s_ss.at[piece, n], s_rs.at[core, (4 - du) % 4, piece],
                        line(core, lax.rem(u + du, 4), v, z, cc),
                    )
                )
        copies.append(
            send(
                sending.at[piece, 1 - core], arrived.at[core, 0, piece], s_ss.at[piece, 0],
                s_rs.at[core, 0, piece], at(x, y, z, 1 - core),
            )
        )

    for du in range(1, 4):
        for cc in range(2):
            wait(hot_in.at[du * 2 + cc], hot_rs.at[du * 2 + cc])
    wait(hot_in.at[1 - core], hot_rs.at[1 - core])

    for piece in range(2):
        for q in range(4 * piece, 4 * piece + 4):
            for j in (1, 3, 2):
                g_wait(q, j)
            unfold(q)
            series(q)
        s_send(piece)
        for q in range(4 * piece, 4 * piece + 4):
            energies(q)

    e_mine[0] = jnp.sum(e_acc[...].T, axis=0, keepdims=True)
    e_local = jnp.logical_and(z_half == 0, core == z_odd)
    e_to = line(core, lax.rem(u + z_half, 4), v, z, z_odd)

    def e_first(act):
        @pl.when(jnp.logical_not(e_local))
        def _():
            act(
                pltpu.make_async_remote_copy(
                    src_ref=e_mine, dst_ref=e_in.at[pl.ds(core, 1)], send_sem=e1_ss,
                    recv_sem=e1_rs.at[core], device_id=e_to, device_id_type=MESH,
                )
            )

    e_first(lambda copy: copy.start())

    @pl.when(e_local)
    def _():
        e_in[core] = e_mine[0]

    def e_second(act):
        @pl.when(owns)
        def _():
            def one(o, _):
                act(
                    pltpu.make_async_remote_copy(
                        src_ref=e_sum, dst_ref=e_all.at[pl.ds(z_half, 1)], send_sem=e2_ss.at[o],
                        recv_sem=e2_rs.at[z_half], device_id=(lax.rem(z + o, 8), ha),
                        device_id_type=MESH,
                    )
                )
                return 0

            lax.fori_loop(1, 8, one, 0)

    def a_wait(piece):
        for half in range(2):
            for du in range(1, 4):
                wait(arrived.at[half, du, piece], s_rs.at[half, du, piece])
        wait(arrived.at[1 - core, 0, piece], s_rs.at[1 - core, 0, piece])

    a_wait(0)

    @pl.when(owns)
    def _():
        for cc in range(2):

            @pl.when(jnp.logical_not(jnp.logical_and(z_half == 0, core == cc)))
            def _():
                wait(e_in.at[pl.ds(cc, 1)], e1_rs.at[cc])

        e_sum[0] = e_in[0] + e_in[1]
        e_all[z_half] = e_sum[0]

    e_second(lambda copy: copy.start())

    a_wait(1)
    for pp in range(8):
        ones = []
        for half in range(2):
            tiles = []
            for n in range(2):
                tiles.append(
                    jnp.concatenate(
                        [
                            arrived[half, i, piece, 2 * pp + n]
                            for i in range(4)
                            for piece in range(2)
                        ],
                        axis=0,
                    )
                )
            ones.append(
                jnp.dot(table[half], jnp.concatenate(tiles, axis=1), preferred_element_type=f32)
            )
        for n in range(2):
            lanes = slice(n * 128, n * 128 + 128)
            for half in range(2):
                real, imag = ones[half][0:128, lanes], ones[half][128:256, lanes]
                c, s = turn_ref[2 * half], turn_ref[2 * half + 1]
                rows = slice((2 * pp + n) * 128, (2 * pp + n) * 128 + 128)
                twiddled[rows, half * 256 : half * 256 + 128] = (real * c + imag * s).astype(bf16)
                twiddled[rows, half * 256 + 128 : half * 256 + 256] = (
                    imag * c - real * s
                ).astype(bf16)

    second = second_ref[...].astype(bf16)
    for chunk in range(4):
        out = jnp.dot(
            twiddled[chunk * 512 : chunk * 512 + 512, :], second, preferred_element_type=f32
        )
        real, imag = out[:, 0:128], out[:, 128:256]
        squares = real * real + imag * imag
        for n in range(4):
            power[pl.ds(4 * chunk + n, 128, stride=16), :] = squares[n * 128 : n * 128 + 128]

    sums = jnp.zeros((HS_DEV, NB), f32)
    for kb in range(32):
        tiles = []
        for pair in range(2):
            base = (kb * 4 + pair * 2) * 16
            even, odd = power[base : base + 16, :], power[base + 16 : base + 32, :]
            tiles.append(
                jnp.concatenate(
                    [jnp.where(left, even, swap(odd)), jnp.where(left, swap(even), odd)], axis=0
                )
            )
        sums = sums + jnp.dot(
            jnp.concatenate(tiles, axis=1).astype(bf16),
            member[kb * 256 : kb * 256 + 256, :],
            preferred_element_type=f32,
        )
    band_ref[...] = sums / (NT * bins)

    for i in range(4):

        @pl.when(jnp.logical_not(jnp.logical_and(owns, z_half == i)))
        def _():
            wait(e_all.at[pl.ds(i, 1)], e2_rs.at[i])

    energy_ref[...] = jnp.sqrt(((e_all[0] + e_all[1]) + (e_all[2] + e_all[3])) / NT + epsilon).reshape(E_DEV)

    for copy in copies:
        copy.wait_send()
    wait(c_out.at[pl.ds(2, 62)], c_ss)
    shape_copies(lambda copy: copy.wait_send())
    e_first(lambda copy: copy.wait_send())
    e_second(lambda copy: copy.wait_send())


def shards(mode_record, mode_shapes, map_elem, map_coef, hot_owner, band_bins):
    f32, bf16 = jnp.float32, jnp.bfloat16
    first, turn, second = tables()
    vmem, dma = pltpu.VMEM, pltpu.SemaphoreType.DMA
    scratch = [
        vmem((HALF, MODES), bf16),
        vmem((MODES, E_DEV), bf16),
        vmem(map_elem.shape, jnp.int32),
        vmem(map_coef.shape, f32),
        vmem((1, HS_DEV), jnp.int32),
        vmem((1, NB), jnp.int32),
        vmem(first.shape, bf16),
        vmem(turn.shape, f32),
        vmem(second.shape, f32),
        vmem((128, 384), f32),
        vmem((384, 384), f32),
        vmem((304, 384), bf16),
        vmem((304, 384), bf16),
        vmem((384, 384), bf16),
        vmem((128, 384), f32),
        vmem((64, 1, 384), f32),
        vmem((64, 1, 384), f32),
        vmem((64, 384), f32),
        vmem((32, 640), bf16),
        vmem((8, 32, 640), bf16),
        vmem((32, FOLD, 128), bf16),
        vmem((8, 640, 256), bf16),
        vmem((2048, 128), f32),
        vmem((2, 8, 16, 16, 128), bf16),
        vmem((2, 4, 2, 16, 16, 128), bf16),
        vmem((NT // 2, NB), bf16),
        vmem((2048, 512), bf16),
        vmem((2048, 128), f32),
        vmem((2, 256, 128), bf16),
        vmem((384, 128), f32),
        vmem((1, 1, 384), f32),
        vmem((2, 1, 384), f32),
        vmem((1, 1, 384), f32),
        vmem((4, 1, 384), f32),
        dma((2,)), dma, dma, dma, dma((8,)), dma((8,)), dma((24,)), dma((32,)), dma((8,)), dma((2,)),
        dma((2, 8)), dma((2, 4, 2)), dma, dma((2,)), dma((8,)), dma((4,)),
        dma((9,)),
    ]
    whole = pl.BlockSpec(memory_space=pltpu.VMEM)
    sums, energy = pl.pallas_call(
        kernel,
        out_shape=(
            pltpu.VMEM((HS_DEV, NB), f32),
            pltpu.VMEM((E_DEV,), f32),
        ),
        in_specs=[pl.BlockSpec(memory_space=pltpu.HBM)] * 9,
        out_specs=(whole, whole),
        scratch_shapes=scratch,
        compiler_params=pltpu.CompilerParams(
            collective_id=0, has_side_effects=True, vmem_limit_bytes=255 * 2**18
        ),
        name="whipping",
    )(
        mode_record.T, mode_shapes, map_elem, map_coef, hot_owner.reshape(1, HS_DEV),
        band_bins.reshape(1, NB), jnp.asarray(first), jnp.asarray(turn), jnp.asarray(second),
    )
    return (energy, sums)


def solution(mesh):
    in_specs = (
        P(None, ("ta", "ha")),
        P(None, "ha"),
        P(None, "ha"),
        P(None, "ha"),
        P(("ta", "ha")),
        P(),
    )
    out_specs = (P("ha"), P(("ta", "ha"), None))
    return jax.shard_map(shards, mesh=mesh, in_specs=in_specs, out_specs=out_specs, check_vma=False)
```

```python
import jax
import jax.numpy as jnp
import numpy as np
from jax import lax
from jax.experimental import pallas as pl
from jax.experimental.pallas import tpu as pltpu
from jax.sharding import PartitionSpec as P

DFT_LEN = 128
NB = 512
K_EXT = 4
HS_DEV = 32
NT = 16384
MODES = 300
E_DEV = 384
FOLD = 160
SPLIT = 96
KPAD = 320
HALF = 64

epsilon = 1e-06
MESH = pl.DeviceIdType.MESH
PLANES = (0, 1, 7, 2, 6, 3, 5, 4)
PLANE_AT = {dz: i for i, dz in enumerate(PLANES)}


def tables():
    import ml_dtypes

    pos = np.arange(DFT_LEN)
    turn = np.float32(2.0 * np.pi / DFT_LEN)
    first = (pos[:, None] * pos[None, :] % DFT_LEN).astype(np.float32) * turn
    first_table = np.concatenate([np.cos(first), -np.sin(first)], axis=0)
    fine = (pos[:, None] * pos[None, :]).astype(np.float32) * np.float32(2.0 * np.pi / NT)
    twiddle = []
    for half in range(2):
        part = fine[:, half * HALF : (half + 1) * HALF]
        part = np.concatenate([part, part], axis=1)
        twiddle += [np.cos(part), np.sin(part)]
    second = np.zeros((4, 2, HALF, 2, 2, HALF), np.float32)
    for half in range(2):
        angles = first[half * HALF : (half + 1) * HALF, :HALF]
        c, s = np.cos(angles), np.sin(angles)
        for hh in range(2):
            second[2 * half, hh, :, 0, hh] = c
            second[2 * half, hh, :, 1, hh] = -s
            second[2 * half + 1, hh, :, 0, hh] = s
            second[2 * half + 1, hh, :, 1, hh] = c
    return (
        first_table.astype(ml_dtypes.bfloat16),
        np.stack(twiddle).astype(np.float32),
        second.reshape(512, 256).astype(ml_dtypes.bfloat16).astype(np.float32),
    )


def kernel(
    rec_hbm, shapes_hbm, elem_hbm, coef_hbm, owner_hbm, bins_hbm, first_hbm, turn_hbm, second_hbm,
    band_ref, energy_ref,
    rec_ref, shapes_ref, elem_ref, coef_ref, owner_ref, bins_ref, first_ref, turn_ref, second_ref,
    pad_rec, pad_shapes, shapes_out, shapes_in, shapes_t,
    c_rows, c_out, c_mid, c_next, c_flat, hot_mine, hot_in,
    gathered, wide, folded, sending, arrived,
    member, twiddled, power, table, e_acc, e_mine, e_in, e_sum, e_all,
    shp_ss, shp_rs, c1_ss, c1_rs, c2_ss, c2_rs, hot_ss, hot_rs, g_ss, g_rs, z_ss, far_rs, h_ss, h_rs, s_ss, s_rs, e1_ss, e1_rs, e2_ss, e2_rs,
    in_sem,
):
    f32, bf16, i32 = jnp.float32, jnp.bfloat16, jnp.int32
    z = lax.axis_index("ta")
    ha = lax.axis_index("ha")
    core = lax.rem(ha, 2)
    x = lax.div(ha, 8)
    y = lax.rem(lax.div(ha, 2), 4)
    u = jnp.where(core == 0, x, y)
    v = jnp.where(core == 0, y, x)
    z_half, z_odd = lax.div(z, 2), lax.rem(z, 2)

    def at(px, py, pz, pc):
        return (pz, (px * 4 + py) * 2 + pc)

    def line(plane_core, pu, pv, pz, pc):
        return at(
            jnp.where(plane_core == 0, pu, pv), jnp.where(plane_core == 0, pv, pu), pz, pc
        )

    def send(src, dst, ss, rs, device):
        copy = pltpu.make_async_remote_copy(
            src_ref=src, dst_ref=dst, send_sem=ss, recv_sem=rs, device_id=device, device_id_type=MESH
        )
        copy.start()
        return copy

    def wait(ref, sem):
        pltpu.make_async_copy(ref, ref, sem).wait()

    fetches = [
        pltpu.make_async_copy(src, dst, in_sem.at[n])
        for n, (src, dst) in enumerate(
            (
                (rec_hbm, rec_ref), (shapes_hbm, shapes_ref), (elem_hbm, elem_ref),
                (coef_hbm, coef_ref), (first_hbm, first_ref), (bins_hbm, bins_ref),
                (owner_hbm, owner_ref), (second_hbm, second_ref), (turn_hbm, turn_ref),
            )
        )
    ]
    for fetch in fetches:
        fetch.start()

    barrier = pltpu.get_barrier_semaphore()

    partners = [at(x, y, lax.rem(z + dz, 8), core) for dz in (1, 7, 2, 6)]
    for d in (1, 3, 2):
        for pc in range(2):
            partners.append(at(x, lax.rem(y + d, 4), z, pc))
            partners.append(at(lax.rem(x + d, 4), y, z, pc))
    partners.append(at(x, y, z, 1 - core))
    for partner in partners:
        pl.semaphore_signal(barrier, inc=1, device_id=partner, device_id_type=MESH)

    lane128 = lax.broadcasted_iota(i32, (1, 128), 1)
    left = lane128 < HALF

    def swap(tile):
        return pltpu.roll(tile, HALF, 1)

    pad_rec[...] = jnp.zeros_like(pad_rec)
    fetches[0].wait()
    pad_rec[0:HALF, 0:MODES] = rec_ref[...].astype(f32)
    turned = pad_rec[...].T
    gathered[0] = (turned[0:FOLD] + swap(turned[FOLD : 2 * FOLD])).astype(bf16)

    shapes_out[MODES - 12 : 304, :] = jnp.zeros((16, E_DEV), bf16)
    for fetch in fetches[1:4]:
        fetch.wait()
    shapes_out[0:MODES, :] = shapes_ref[...]
    slots = pl.ds(pl.multiple_of(z_half * 128, 128), 128)
    elems = elem_ref[:, slots]
    coefs = coef_ref[:, slots]
    elem_ids = lax.broadcasted_iota(i32, (E_DEV, 128), 0)
    hot = jnp.zeros((304, 128), f32)
    for k in range(K_EXT):
        pick = (elem_ids == elems[k : k + 1, :]).astype(f32).astype(bf16)
        hot = hot + coefs[k : k + 1, :] * jnp.dot(
            shapes_out[...], pick, preferred_element_type=f32
        )
    hot = jnp.concatenate([hot, jnp.zeros((80, 128), f32)], axis=0).T
    for t in range(3):
        c_rows[t * 128 : t * 128 + 128, :] = hot[:, t * 128 : t * 128 + 128]

    for g in range(8):
        for t in range(3):
            for rank in range(2):
                start = t * 128 + z_odd * HALF + 16 * (g // 2) + 2 * (g % 2) + rank
                to = (g * 3 + t) * 8 + rank * 4
                c_out[to : to + 4, :] = c_rows[pl.ds(start, 4, stride=4), :]

    col = lax.broadcasted_iota(i32, (128, 128), 1)
    row = lax.broadcasted_iota(i32, (128, 128), 0)
    source, place, dv = lax.div(col, 32), lax.div(lax.rem(col, 32), 4), lax.rem(col, 4)
    dz = jnp.zeros_like(col)
    for i, value in enumerate(PLANES):
        dz = jnp.where(place == i, value, dz)
    zz = lax.rem(z + dz, 8)
    a_even = 16 * zz + 4 * lax.rem(x + source, 4) + lax.rem(y + dv, 4)
    a_odd = 16 * zz + 4 * lax.rem(x + dv, 4) + lax.rem(y + source, 4)
    fetches[4].wait()
    for half, a_of in enumerate((a_even, a_odd)):
        order = (row == a_of).astype(f32).astype(bf16)
        table[half] = jnp.dot(first_ref[...], order, preferred_element_type=f32).astype(bf16)

    for fetch in fetches[5:]:
        fetch.wait()
    bins = bins_ref[...].astype(f32)
    before = (
        lax.broadcasted_iota(i32, (NB, NB), 0) < lax.broadcasted_iota(i32, (NB, NB), 1)
    ).astype(f32).astype(bf16)
    starts = jnp.dot(
        jnp.broadcast_to(bins, (8, NB)).astype(bf16), before, preferred_element_type=f32
    )[0:1]
    starts_i = starts.astype(i32)
    ends_i = (starts + bins).astype(i32)

    def member_block(i, _):
        rows = lax.broadcasted_iota(i32, (256, 1), 0)
        bin_ids = i * 4 + lax.div(rows, HALF) + DFT_LEN * lax.rem(rows, HALF)
        inside = jnp.logical_and(bin_ids >= starts_i, bin_ids < ends_i)
        member[pl.ds(pl.multiple_of(i * 256, 256), 256), :] = inside.astype(f32).astype(bf16)
        return 0

    pl.semaphore_wait(barrier, len(partners))

    copies = []

    first_rows, last_rows = pl.ds(0, SPLIT), pl.ds(SPLIT, FOLD - SPLIT)

    def a_wait_first(q, j):
        wait(gathered.at[q * 4 + j, first_rows], g_rs.at[q * 4 + j])

    def a_wait_last(q, j):
        wait(gathered.at[q * 4 + j, last_rows], h_rs.at[q * 4 + j])

    def v_send(q):
        for j in (1, 3, 2):
            copies.append(
                send(
                    gathered.at[q * 4, first_rows], gathered.at[q * 4 + j, first_rows],
                    g_ss.at[3 * q + j - 1], g_rs.at[q * 4 + j],
                    line(core, u, lax.rem(v + 4 - j, 4), z, core),
                )
            )

    def z_send(n, q, dq, dz, rows=None):
        src, dst = gathered.at[q * 4, first_rows], gathered.at[dq * 4, first_rows]
        rs = g_rs.at[dq * 4]
        if rows is not None:
            part = pl.ds(rows * (SPLIT // 2), SPLIT // 2)
            src, dst, rs = gathered.at[q * 4, part], gathered.at[dq * 4, part], far_rs.at[rows]
        copies.append(send(src, dst, z_ss.at[n], rs, at(x, y, lax.rem(z + 8 + dz, 8), core)))

    def last_v_send():
        for j in (1, 3, 2):
            copies.append(
                send(
                    gathered.at[0, last_rows], gathered.at[j, last_rows], h_ss.at[j - 1],
                    h_rs.at[j], line(core, u, lax.rem(v + 4 - j, 4), z, core),
                )
            )

    last_count = [3]

    def last_z_send(dz, to, j):
        q, dq = PLANE_AT[dz % 8], PLANE_AT[(dz - to) % 8]
        n = last_count[0]
        last_count[0] += 1
        copies.append(
            send(
                gathered.at[q * 4 + j, last_rows], gathered.at[dq * 4 + j, last_rows], h_ss.at[n],
                h_rs.at[dq * 4 + j], at(x, y, lax.rem(z + 8 + to, 8), core),
            )
        )

    def last_near(j):
        for to in (1, -1, 2, -2):
            last_z_send(0, to, j)

    def last_far(j):
        a_wait_last(PLANE_AT[2], j)
        last_z_send(2, -1, j)
        if j in (0, 1):
            last_z_send(2, -2, j)
        a_wait_last(PLANE_AT[6], j)
        last_z_send(-2, 1, j)
        if j in (2, 3):
            last_z_send(-2, 2, j)

    def group(px, pc):
        return pl.ds(pl.multiple_of(24 * (px * 2 + pc), 8), 24)

    for dx in (1, 3, 2, 0):
        for dc in range(2):
            to_x, to_c = lax.rem(x + dx, 4), jnp.where(dc == 0, core, 1 - core)
            if dx or dc:
                g = ((4 - dx) % 4) * 2 + dc
                send(
                    c_out.at[group(to_x, to_c)], c_mid.at[pl.ds(24 * g, 24)], c1_ss, c1_rs,
                    at(to_x, y, z, to_c),
                )
    c_mid[0:24, :] = c_out[group(x, core), :]

    for n, dz in enumerate((1, 7, 2, 6)):
        z_send(n, 0, PLANE_AT[dz], -dz)
    last_v_send()
    last_near(0)
    v_send(0)

    def c_pass():
        wait(c_mid.at[pl.ds(24, 168)], c1_rs)
        for dy in (1, 3, 2, 0):
            to_y = lax.rem(y + dy, 4)
            for t in range(3):
                for rank in range(2):
                    to = dy * 48 + t * 16 + rank * 8
                    c_next[to : to + 8, :] = c_mid[
                        pl.ds(t * 8 + rank * 4 + to_y, 8, stride=24), :
                    ]
            if dy:
                send(
                    c_next.at[pl.ds(dy * 48, 48)], c_flat.at[pl.ds((4 - dy) * 48, 48)], c2_ss,
                    c2_rs, at(x, to_y, z, core),
                )
        c_flat[0:48, :] = c_next[0:48, :]

    owns = core == z_odd
    shp_to = [
        line(0, lax.rem(x + 4 - z_half, 4), y, z, 0),
        line(1, lax.rem(y + 4 - z_half, 4), x, z, 1),
    ]

    def shape_copies(act):
        for cc in range(2):
            own_work = jnp.logical_and(z_half == 0, core == cc)

            @pl.when(jnp.logical_and(owns, jnp.logical_not(own_work)))
            def _():
                act(
                    pltpu.make_async_remote_copy(
                        src_ref=shapes_out, dst_ref=shapes_in, send_sem=shp_ss.at[cc],
                        recv_sem=shp_rs, device_id=shp_to[cc], device_id_type=MESH,
                    )
                )

    shape_copies(lambda copy: copy.start())
    local_shapes = jnp.logical_and(owns, z_half == 0)

    @pl.when(local_shapes)
    def _():
        shapes_in[...] = shapes_out[...]

    for j in (1, 3, 2):
        a_wait_last(0, j)
        last_near(j)
    for q in (PLANE_AT[1], PLANE_AT[7]):
        a_wait_first(q, 0)
        v_send(q)
    c_pass()
    for n, (dz, step) in enumerate(((2, -1), (6, 1))):
        q = PLANE_AT[dz]
        a_wait_first(q, 0)
        z_send(4 + 2 * n, q, PLANE_AT[(dz - step) % 8], step)
        z_send(5 + 2 * n, q, PLANE_AT[4], 2 * step, n)
        v_send(q)
    last_far(0)
    wait(c_flat.at[pl.ds(48, 144)], c2_rs)
    owner_row = owner_ref[...]
    r32 = lax.broadcasted_iota(i32, (32, 32), 0)
    c32 = lax.broadcasted_iota(i32, (32, 32), 1)
    owners = jnp.broadcast_to(owner_row, (32, 32))
    owner_col = jnp.sum(jnp.where(r32 == c32, owners, 0), axis=1, keepdims=True)
    rank = jnp.sum(
        jnp.logical_and(owners == owner_col, c32 < r32).astype(i32), axis=1, keepdims=True
    )
    slot = lax.broadcasted_iota(i32, (32, 64), 1)
    region_x = lax.rem(x + lax.rem(lax.div(slot, 2), 4), 4)
    region_y = lax.rem(y + lax.div(slot, 16), 4)
    region_c = lax.rem(core + lax.rem(slot, 2), 2)
    region = (region_x * 4 + region_y) * 2 + region_c
    chosen = jnp.logical_and(region == owner_col, lax.rem(lax.div(slot, 8), 2) == rank)
    chosen = chosen.astype(f32).astype(bf16)
    flat = jnp.concatenate(
        [
            jnp.concatenate(
                [c_flat[e * 48 + t * 16 : e * 48 + t * 16 + 16, :] for e in range(4)], axis=0
            )
            for t in range(3)
        ],
        axis=1,
    )
    high = flat.astype(bf16)
    low = (flat - high.astype(f32)).astype(bf16)
    high = jnp.dot(chosen, high, preferred_element_type=f32)
    low = jnp.dot(chosen, low, preferred_element_type=f32)
    hot_mine[...] = jnp.concatenate(
        [high[:, 0:256], high[:, 256:384] + swap(low[:, 256:384]), low[:, 0:256]], axis=1
    ).astype(bf16)
    hot_in[core] = hot_mine[...]
    for du in range(1, 4):
        for cc in range(2):
            here_u, here_v = (x, y) if cc == 0 else (y, x)
            copies.append(
                send(
                    hot_mine, hot_in.at[du * 2 + core], hot_ss.at[du * 2 + cc],
                    hot_rs.at[du * 2 + core], line(cc, lax.rem(here_u + 4 - du, 4), here_v, z, cc),
                )
            )
    copies.append(
        send(hot_mine, hot_in.at[core], hot_ss.at[0], hot_rs.at[core], at(x, y, z, 1 - core))
    )


    for q in (PLANE_AT[3], PLANE_AT[5]):
        a_wait_first(q, 0)
        v_send(q)
    for n in range(2):
        part = pl.ds(n * (SPLIT // 2), SPLIT // 2)
        wait(gathered.at[PLANE_AT[4] * 4, part], far_rs.at[n])
    v_send(PLANE_AT[4])
    for j in (1, 3, 2):
        last_far(j)
    @pl.when(jnp.logical_not(local_shapes))
    def _():
        wait(shapes_in, shp_rs)

    pad_shapes[0:304, :] = shapes_in[...].astype(f32)
    pad_shapes[304:384, :] = jnp.zeros((80, E_DEV), f32)
    shapes_t[...] = pad_shapes[...].T.astype(bf16)
    e_acc[...] = jnp.zeros_like(e_acc)

    def unfold(q):
        parts = []
        for pair in range(2):
            even = gathered[q * 4 + 2 * pair].astype(f32)
            odd = gathered[q * 4 + 2 * pair + 1].astype(f32)
            parts.append(
                (
                    jnp.where(left, even, swap(odd)).astype(bf16),
                    jnp.where(left, swap(even), odd).astype(bf16),
                )
            )
        first = jnp.concatenate([parts[0][0], parts[1][0]], axis=1)
        last = jnp.concatenate([parts[0][1], parts[1][1]], axis=1)
        wide[q, 0:160, :] = first
        wide[q, 160:320, :] = last
        wide[q, 320:384, :] = last[96:160]
        wide[q, 384:544, :] = first
        wide[q, 544:640, :] = last[0:96]

    def energies(q):
        stress = jnp.dot(shapes_t[...], wide[q, 0:384, :], preferred_element_type=f32)
        squares = stress * stress
        e_acc[...] += squares[:, 0:128] + squares[:, 128:256]

    def series(q):
        out = jnp.dot(
            hot_in[...].reshape(256, 640), wide[q], preferred_element_type=f32
        ).reshape(8, 2, 16, 256)
        for pair in range(2):
            lanes = slice(pair * 128, pair * 128 + 128)
            top = out[:, 0, :, lanes].reshape(128, 128)
            low_half = out[:, 1, :, lanes].reshape(128, 128)
            for n, tile in enumerate(
                (
                    jnp.where(left, top, swap(low_half)),
                    jnp.where(left, swap(top), low_half),
                )
            ):
                folded[pl.ds((q % 4) * 4 + pair * 2 + n, 128, stride=16), :] = tile

    def s_send(piece):
        sending[piece] = folded[...].astype(bf16).reshape(8, 16, 16, 128)
        arrived[core, 0, piece] = sending[piece, core]
        for du in range(1, 4):
            for cc in range(2):
                n = du * 2 + cc
                copies.append(
                    send(
                        sending.at[piece, n], arrived.at[core, (4 - du) % 4, piece],
                        s_ss.at[piece, n], s_rs.at[core, (4 - du) % 4, piece],
                        line(core, lax.rem(u + du, 4), v, z, cc),
                    )
                )
        copies.append(
            send(
                sending.at[piece, 1 - core], arrived.at[core, 0, piece], s_ss.at[piece, 0],
                s_rs.at[core, 0, piece], at(x, y, z, 1 - core),
            )
        )

    def planes(piece):
        for q in range(4 * piece, 4 * piece + 4):
            for j in range(4):
                if j:
                    a_wait_first(q, j)
                if q not in (PLANE_AT[0], PLANE_AT[2], PLANE_AT[6]):
                    a_wait_last(q, j)
            unfold(q)
            energies(q)

    planes(0)
    for du in range(1, 4):
        for cc in range(2):
            wait(hot_in.at[du * 2 + cc], hot_rs.at[du * 2 + cc])
    wait(hot_in.at[1 - core], hot_rs.at[1 - core])

    for q in range(4):
        series(q)
    s_send(0)
    planes(1)

    e_mine[0] = jnp.sum(e_acc[...].T, axis=0, keepdims=True)
    e_local = jnp.logical_and(z_half == 0, core == z_odd)
    e_to = line(core, lax.rem(u + z_half, 4), v, z, z_odd)

    def e_first(act):
        @pl.when(jnp.logical_not(e_local))
        def _():
            act(
                pltpu.make_async_remote_copy(
                    src_ref=e_mine, dst_ref=e_in.at[pl.ds(core, 1)], send_sem=e1_ss,
                    recv_sem=e1_rs.at[core], device_id=e_to, device_id_type=MESH,
                )
            )

    e_first(lambda copy: copy.start())

    @pl.when(e_local)
    def _():
        e_in[core] = e_mine[0]

    def a_wait(piece):
        for half in range(2):
            for du in range(1, 4):
                wait(arrived.at[half, du, piece], s_rs.at[half, du, piece])
        wait(arrived.at[1 - core, 0, piece], s_rs.at[1 - core, 0, piece])

    for q in range(4, 8):
        series(q)
    s_send(1)

    def e_slot(d):
        return lax.div(lax.rem(z + d, 8), 2)

    def e_wait(d):
        wait(e_all.at[pl.ds(e_slot(d), 1)], e2_rs.at[e_slot(d)])

    def e_copy(src, d, to, n):
        return pltpu.make_async_remote_copy(
            src_ref=src, dst_ref=e_all.at[pl.ds(e_slot(d), 1)], send_sem=e2_ss.at[n],
            recv_sem=e2_rs.at[e_slot(d)], device_id=at(x, y, lax.rem(z + to, 8), core),
            device_id_type=MESH,
        )

    def e_second(act):
        @pl.when(owns)
        def _():
            for n, to in enumerate((1, 7, 2, 6)):
                act(e_copy(e_sum, 0, to, n))

    def e_third(act):
        @pl.when(owns)
        def _():
            act(e_copy(e_all.at[pl.ds(e_slot(2), 1)], 2, 6, 4))

        @pl.when(jnp.logical_not(owns))
        def _():
            act(e_copy(e_all.at[pl.ds(e_slot(1), 1)], 1, 6, 4))
            act(e_copy(e_all.at[pl.ds(e_slot(7), 1)], 7, 2, 5))

    lax.fori_loop(0, 16, member_block, 0)

    @pl.when(owns)
    def _():
        for cc in range(2):

            @pl.when(jnp.logical_not(jnp.logical_and(z_half == 0, core == cc)))
            def _():
                wait(e_in.at[pl.ds(cc, 1)], e1_rs.at[cc])

        e_sum[0] = e_in[0] + e_in[1]
        e_all[z_half] = e_sum[0]

    e_second(lambda copy: copy.start())
    lax.fori_loop(16, 32, member_block, 0)
    a_wait(0)
    @pl.when(owns)
    def _():
        e_wait(2)

    @pl.when(jnp.logical_not(owns))
    def _():
        e_wait(1)
        e_wait(7)

    e_third(lambda copy: copy.start())

    a_wait(1)
    for pp in range(8):
        ones = []
        for half in range(2):
            tiles = []
            for n in range(2):
                tiles.append(
                    jnp.concatenate(
                        [
                            arrived[half, i, piece, 2 * pp + n]
                            for i in range(4)
                            for piece in range(2)
                        ],
                        axis=0,
                    )
                )
            ones.append(
                jnp.dot(table[half], jnp.concatenate(tiles, axis=1), preferred_element_type=f32)
            )
        for n in range(2):
            lanes = slice(n * 128, n * 128 + 128)
            for half in range(2):
                real, imag = ones[half][0:128, lanes], ones[half][128:256, lanes]
                c, s = turn_ref[2 * half], turn_ref[2 * half + 1]
                rows = slice((2 * pp + n) * 128, (2 * pp + n) * 128 + 128)
                twiddled[rows, half * 256 : half * 256 + 128] = (real * c + imag * s).astype(bf16)
                twiddled[rows, half * 256 + 128 : half * 256 + 256] = (
                    imag * c - real * s
                ).astype(bf16)

    second = second_ref[...].astype(bf16)
    for chunk in range(4):
        out = jnp.dot(
            twiddled[chunk * 512 : chunk * 512 + 512, :], second, preferred_element_type=f32
        )
        real, imag = out[:, 0:128], out[:, 128:256]
        squares = real * real + imag * imag
        for n in range(4):
            power[pl.ds(4 * chunk + n, 128, stride=16), :] = squares[n * 128 : n * 128 + 128]

    sums = jnp.zeros((HS_DEV, NB), f32)
    for kb in range(32):
        tiles = []
        for pair in range(2):
            base = (kb * 4 + pair * 2) * 16
            even, odd = power[base : base + 16, :], power[base + 16 : base + 32, :]
            tiles.append(
                jnp.concatenate(
                    [jnp.where(left, even, swap(odd)), jnp.where(left, swap(even), odd)], axis=0
                )
            )
        sums = sums + jnp.dot(
            jnp.concatenate(tiles, axis=1).astype(bf16),
            member[kb * 256 : kb * 256 + 256, :],
            preferred_element_type=f32,
        )
    band_ref[...] = sums / (NT * bins)

    @pl.when(owns)
    def _():
        e_wait(6)
        e_wait(4)

    @pl.when(jnp.logical_not(owns))
    def _():
        e_wait(3)
        e_wait(5)

    energy_ref[...] = jnp.sqrt(((e_all[0] + e_all[1]) + (e_all[2] + e_all[3])) / NT + epsilon).reshape(E_DEV)

    for copy in copies:
        copy.wait_send()
    wait(c_out.at[pl.ds(24, 168)], c1_ss)
    wait(c_next.at[pl.ds(48, 144)], c2_ss)
    shape_copies(lambda copy: copy.wait_send())
    e_first(lambda copy: copy.wait_send())
    e_second(lambda copy: copy.wait_send())
    e_third(lambda copy: copy.wait_send())


def shards(mode_record, mode_shapes, map_elem, map_coef, hot_owner, band_bins):
    f32, bf16 = jnp.float32, jnp.bfloat16
    first, turn, second = tables()
    vmem, dma = pltpu.VMEM, pltpu.SemaphoreType.DMA
    scratch = [
        vmem((HALF, MODES), bf16),
        vmem((MODES, E_DEV), bf16),
        vmem(map_elem.shape, jnp.int32),
        vmem(map_coef.shape, f32),
        vmem((1, HS_DEV), jnp.int32),
        vmem((1, NB), jnp.int32),
        vmem(first.shape, bf16),
        vmem(turn.shape, f32),
        vmem(second.shape, f32),
        vmem((128, 384), f32),
        vmem((384, 384), f32),
        vmem((304, 384), bf16),
        vmem((304, 384), bf16),
        vmem((384, 384), bf16),
        vmem((384, 128), f32),
        vmem((192, 128), f32),
        vmem((192, 128), f32),
        vmem((192, 128), f32),
        vmem((192, 128), f32),
        vmem((32, 640), bf16),
        vmem((8, 32, 640), bf16),
        vmem((32, FOLD, 128), bf16),
        vmem((8, 640, 256), bf16),
        vmem((2048, 128), f32),
        vmem((2, 8, 16, 16, 128), bf16),
        vmem((2, 4, 2, 16, 16, 128), bf16),
        vmem((NT // 2, NB), bf16),
        vmem((2048, 512), bf16),
        vmem((2048, 128), f32),
        vmem((2, 256, 128), bf16),
        vmem((384, 128), f32),
        vmem((1, 1, 384), f32),
        vmem((2, 1, 384), f32),
        vmem((1, 1, 384), f32),
        vmem((4, 1, 384), f32),
        dma((2,)), dma, dma, dma, dma, dma, dma((8,)), dma((8,)), dma((24,)), dma((32,)), dma((8,)), dma((2,)), dma((31,)), dma((32,)),
        dma((2, 8)), dma((2, 4, 2)), dma, dma((2,)), dma((8,)), dma((4,)),
        dma((9,)),
    ]
    whole = pl.BlockSpec(memory_space=pltpu.VMEM)
    sums, energy = pl.pallas_call(
        kernel,
        out_shape=(
            pltpu.VMEM((HS_DEV, NB), f32),
            pltpu.VMEM((E_DEV,), f32),
        ),
        in_specs=[pl.BlockSpec(memory_space=pltpu.HBM)] * 9,
        out_specs=(whole, whole),
        scratch_shapes=scratch,
        compiler_params=pltpu.CompilerParams(
            collective_id=0, has_side_effects=True, vmem_limit_bytes=255 * 2**18
        ),
        name="whipping",
    )(
        mode_record.T, mode_shapes, map_elem, map_coef, hot_owner.reshape(1, HS_DEV),
        band_bins.reshape(1, NB), jnp.asarray(first), jnp.asarray(turn), jnp.asarray(second),
    )
    return (energy, sums)


def solution(mesh):
    in_specs = (
        P(None, ("ta", "ha")),
        P(None, "ha"),
        P(None, "ha"),
        P(None, "ha"),
        P(("ta", "ha")),
        P(),
    )
    out_specs = (P("ha"), P(("ta", "ha"), None))
    return jax.shard_map(shards, mesh=mesh, in_specs=in_specs, out_specs=out_specs, check_vma=False)
```

```python
import jax
import jax.numpy as jnp
import numpy as np
from jax import lax
from jax.experimental import pallas as pl
from jax.experimental.pallas import tpu as pltpu
from jax.sharding import PartitionSpec as P

DFT_LEN = 128
NB = 512
K_EXT = 4
HS_DEV = 32
NT = 16384
MODES = 300
E_DEV = 384
FOLD = 160
SPLIT = 96
KPAD = 320
HALF = 64

epsilon = 1e-06
MESH = pl.DeviceIdType.MESH
PLANES = (0, 1, 7, 2, 6, 3, 5, 4)
PLANE_AT = {dz: i for i, dz in enumerate(PLANES)}


def tables():
    import ml_dtypes

    pos = np.arange(DFT_LEN)
    turn = np.float32(2.0 * np.pi / DFT_LEN)
    first = (pos[:, None] * pos[None, :] % DFT_LEN).astype(np.float32) * turn
    first_table = np.concatenate([np.cos(first), -np.sin(first)], axis=0)
    fine = (pos[:, None] * pos[None, :]).astype(np.float32) * np.float32(2.0 * np.pi / NT)
    twiddle = []
    for half in range(2):
        part = fine[:, half * HALF : (half + 1) * HALF]
        part = np.concatenate([part, part], axis=1)
        twiddle += [np.cos(part), np.sin(part)]
    second = np.zeros((4, 2, HALF, 2, 2, HALF), np.float32)
    for half in range(2):
        angles = first[half * HALF : (half + 1) * HALF, :HALF]
        c, s = np.cos(angles), np.sin(angles)
        for hh in range(2):
            second[2 * half, hh, :, 0, hh] = c
            second[2 * half, hh, :, 1, hh] = -s
            second[2 * half + 1, hh, :, 0, hh] = s
            second[2 * half + 1, hh, :, 1, hh] = c
    return (
        first_table.astype(ml_dtypes.bfloat16),
        np.stack(twiddle).astype(np.float32),
        second.reshape(512, 256).astype(ml_dtypes.bfloat16).astype(np.float32),
    )


def kernel(
    rec_hbm, shapes_hbm, elem_hbm, coef_hbm, owner_hbm, bins_hbm, first_hbm, turn_hbm, second_hbm,
    band_ref, energy_ref,
    rec_ref, shapes_ref, elem_ref, coef_ref, owner_ref, bins_ref, first_ref, turn_ref, second_ref,
    pad_rec, pad_shapes, shapes_out, shapes_in, shapes_t,
    c_rows, c_out, c_mid, c_next, c_flat, hot_mine, hot_in,
    gathered, wide, folded, sending, arrived,
    member, twiddled, power, table, e_acc, e_mine, e_in, e_sum, e_all,
    shp_ss, shp_rs, c1_ss, c1_rs, c2_ss, c2_rs, hot_ss, hot_rs, g_ss, g_rs, z_ss, far_rs, h_ss, h_rs, s_ss, s_rs, e1_ss, e1_rs, e2_ss, e2_rs,
    in_sem,
):
    f32, bf16, i32 = jnp.float32, jnp.bfloat16, jnp.int32
    z = lax.axis_index("ta")
    ha = lax.axis_index("ha")
    core = lax.rem(ha, 2)
    x = lax.div(ha, 8)
    y = lax.rem(lax.div(ha, 2), 4)
    u = jnp.where(core == 0, x, y)
    v = jnp.where(core == 0, y, x)
    z_half, z_odd = lax.div(z, 2), lax.rem(z, 2)

    def at(px, py, pz, pc):
        return (pz, (px * 4 + py) * 2 + pc)

    def line(plane_core, pu, pv, pz, pc):
        return at(
            jnp.where(plane_core == 0, pu, pv), jnp.where(plane_core == 0, pv, pu), pz, pc
        )

    def send(src, dst, ss, rs, device):
        copy = pltpu.make_async_remote_copy(
            src_ref=src, dst_ref=dst, send_sem=ss, recv_sem=rs, device_id=device, device_id_type=MESH
        )
        copy.start()
        return copy

    def wait(ref, sem):
        pltpu.make_async_copy(ref, ref, sem).wait()

    fetches = [
        pltpu.make_async_copy(src, dst, in_sem.at[n])
        for n, (src, dst) in enumerate(
            (
                (rec_hbm, rec_ref), (shapes_hbm, shapes_ref), (elem_hbm, elem_ref),
                (coef_hbm, coef_ref), (first_hbm, first_ref), (bins_hbm, bins_ref),
                (owner_hbm, owner_ref), (second_hbm, second_ref), (turn_hbm, turn_ref),
            )
        )
    ]
    for fetch in fetches:
        fetch.start()

    barrier = pltpu.get_barrier_semaphore()

    partners = [at(x, y, lax.rem(z + dz, 8), core) for dz in (1, 7, 2, 6)]
    for d in (1, 3, 2):
        for pc in range(2):
            partners.append(at(x, lax.rem(y + d, 4), z, pc))
            partners.append(at(lax.rem(x + d, 4), y, z, pc))
    partners.append(at(x, y, z, 1 - core))
    for partner in partners:
        pl.semaphore_signal(barrier, inc=1, device_id=partner, device_id_type=MESH)

    lane128 = lax.broadcasted_iota(i32, (1, 128), 1)
    left = lane128 < HALF

    def swap(tile):
        return pltpu.roll(tile, HALF, 1)

    pad_rec[...] = jnp.zeros_like(pad_rec)
    fetches[0].wait()
    pad_rec[0:HALF, 0:MODES] = rec_ref[...].astype(f32)
    turned = pad_rec[...].T
    gathered[0] = (turned[0:FOLD] + swap(turned[FOLD : 2 * FOLD])).astype(bf16)

    shapes_out[MODES - 12 : 304, :] = jnp.zeros((16, E_DEV), bf16)
    for fetch in fetches[1:4]:
        fetch.wait()
    shapes_out[0:MODES, :] = shapes_ref[...]
    slots = pl.ds(pl.multiple_of(z_half * 128, 128), 128)
    elems = elem_ref[:, slots]
    coefs = coef_ref[:, slots]
    elem_ids = lax.broadcasted_iota(i32, (E_DEV, 128), 0)
    hot = jnp.zeros((304, 128), f32)
    for k in range(K_EXT):
        pick = (elem_ids == elems[k : k + 1, :]).astype(f32).astype(bf16)
        hot = hot + coefs[k : k + 1, :] * jnp.dot(
            shapes_out[...], pick, preferred_element_type=f32
        )
    hot = jnp.concatenate([hot, jnp.zeros((80, 128), f32)], axis=0).T
    for t in range(3):
        c_rows[t * 128 : t * 128 + 128, :] = hot[:, t * 128 : t * 128 + 128]

    for g in range(8):
        for t in range(3):
            for rank in range(2):
                start = t * 128 + z_odd * HALF + 16 * (g // 2) + 2 * (g % 2) + rank
                to = (g * 3 + t) * 8 + rank * 4
                c_out[to : to + 4, :] = c_rows[pl.ds(start, 4, stride=4), :]

    col = lax.broadcasted_iota(i32, (128, 128), 1)
    row = lax.broadcasted_iota(i32, (128, 128), 0)
    source, place, dv = lax.div(col, 32), lax.div(lax.rem(col, 32), 4), lax.rem(col, 4)
    dz = jnp.zeros_like(col)
    for i, value in enumerate(PLANES):
        dz = jnp.where(place == i, value, dz)
    zz = lax.rem(z + dz, 8)
    a_even = 16 * zz + 4 * lax.rem(x + source, 4) + lax.rem(y + dv, 4)
    a_odd = 16 * zz + 4 * lax.rem(x + dv, 4) + lax.rem(y + source, 4)
    fetches[4].wait()
    for half, a_of in enumerate((a_even, a_odd)):
        order = (row == a_of).astype(f32).astype(bf16)
        table[half] = jnp.dot(first_ref[...], order, preferred_element_type=f32).astype(bf16)

    for fetch in fetches[5:]:
        fetch.wait()
    bins = bins_ref[...].astype(f32)
    before = (
        lax.broadcasted_iota(i32, (NB, NB), 0) < lax.broadcasted_iota(i32, (NB, NB), 1)
    ).astype(f32).astype(bf16)
    starts = jnp.dot(
        jnp.broadcast_to(bins, (8, NB)).astype(bf16), before, preferred_element_type=f32
    )[0:1]
    starts_i = starts.astype(i32)
    ends_i = (starts + bins).astype(i32)

    def member_block(i, _):
        rows = lax.broadcasted_iota(i32, (256, 1), 0)
        bin_ids = i * 4 + lax.div(rows, HALF) + DFT_LEN * lax.rem(rows, HALF)
        inside = jnp.logical_and(bin_ids >= starts_i, bin_ids < ends_i)
        member[pl.ds(pl.multiple_of(i * 256, 256), 256), :] = inside.astype(f32).astype(bf16)
        return 0

    pl.semaphore_wait(barrier, len(partners))

    copies = []

    first_rows, last_rows = pl.ds(0, SPLIT), pl.ds(SPLIT, FOLD - SPLIT)

    def a_wait_first(q, j):
        wait(gathered.at[q * 4 + j, first_rows], g_rs.at[q * 4 + j])

    def a_wait_last(q, j):
        wait(gathered.at[q * 4 + j, last_rows], h_rs.at[q * 4 + j])

    def v_send(q):
        for j in (2, 1, 3):
            copies.append(
                send(
                    gathered.at[q * 4, first_rows], gathered.at[q * 4 + j, first_rows],
                    g_ss.at[3 * q + j - 1], g_rs.at[q * 4 + j],
                    line(core, u, lax.rem(v + 4 - j, 4), z, core),
                )
            )

    def z_send(n, q, dq, dz, rows=None):
        src, dst = gathered.at[q * 4, first_rows], gathered.at[dq * 4, first_rows]
        rs = g_rs.at[dq * 4]
        if rows is not None:
            part = pl.ds(rows * (SPLIT // 2), SPLIT // 2)
            src, dst, rs = gathered.at[q * 4, part], gathered.at[dq * 4, part], far_rs.at[rows]
        copies.append(send(src, dst, z_ss.at[n], rs, at(x, y, lax.rem(z + 8 + dz, 8), core)))

    def last_v_send():
        for j in (2, 1, 3):
            copies.append(
                send(
                    gathered.at[0, last_rows], gathered.at[j, last_rows], h_ss.at[j - 1],
                    h_rs.at[j], line(core, u, lax.rem(v + 4 - j, 4), z, core),
                )
            )

    last_count = [3]

    def last_z_send(dz, to, j):
        q, dq = PLANE_AT[dz % 8], PLANE_AT[(dz - to) % 8]
        n = last_count[0]
        last_count[0] += 1
        copies.append(
            send(
                gathered.at[q * 4 + j, last_rows], gathered.at[dq * 4 + j, last_rows], h_ss.at[n],
                h_rs.at[dq * 4 + j], at(x, y, lax.rem(z + 8 + to, 8), core),
            )
        )

    def last_near(j):
        for to in (1, -1, 2, -2):
            last_z_send(0, to, j)

    def last_far(j):
        a_wait_last(PLANE_AT[2], j)
        last_z_send(2, -1, j)
        if j in (0, 1):
            last_z_send(2, -2, j)
        a_wait_last(PLANE_AT[6], j)
        last_z_send(-2, 1, j)
        if j in (2, 3):
            last_z_send(-2, 2, j)

    def group(px, pc):
        return pl.ds(pl.multiple_of(24 * (px * 2 + pc), 8), 24)

    for dx in (2, 1, 3, 0):
        for dc in range(2):
            to_x, to_c = lax.rem(x + dx, 4), jnp.where(dc == 0, core, 1 - core)
            if dx or dc:
                g = ((4 - dx) % 4) * 2 + dc
                send(
                    c_out.at[group(to_x, to_c)], c_mid.at[pl.ds(24 * g, 24)], c1_ss, c1_rs,
                    at(to_x, y, z, to_c),
                )
    c_mid[0:24, :] = c_out[group(x, core), :]

    for n, dz in enumerate((1, 7, 2, 6)):
        z_send(n, 0, PLANE_AT[dz], -dz)
    last_v_send()
    last_near(0)
    v_send(0)

    def c_pass():
        wait(c_mid.at[pl.ds(24, 168)], c1_rs)
        for dy in (2, 1, 3, 0):
            to_y = lax.rem(y + dy, 4)
            for t in range(3):
                for rank in range(2):
                    to = dy * 48 + t * 16 + rank * 8
                    c_next[to : to + 8, :] = c_mid[
                        pl.ds(t * 8 + rank * 4 + to_y, 8, stride=24), :
                    ]
            if dy:
                send(
                    c_next.at[pl.ds(dy * 48, 48)], c_flat.at[pl.ds((4 - dy) * 48, 48)], c2_ss,
                    c2_rs, at(x, to_y, z, core),
                )
        c_flat[0:48, :] = c_next[0:48, :]

    owns = core == z_odd
    shp_to = [
        line(0, lax.rem(x + 4 - z_half, 4), y, z, 0),
        line(1, lax.rem(y + 4 - z_half, 4), x, z, 1),
    ]

    def shape_copies(act):
        for cc in range(2):
            own_work = jnp.logical_and(z_half == 0, core == cc)

            @pl.when(jnp.logical_and(owns, jnp.logical_not(own_work)))
            def _():
                act(
                    pltpu.make_async_remote_copy(
                        src_ref=shapes_out, dst_ref=shapes_in, send_sem=shp_ss.at[cc],
                        recv_sem=shp_rs, device_id=shp_to[cc], device_id_type=MESH,
                    )
                )

    shape_copies(lambda copy: copy.start())
    local_shapes = jnp.logical_and(owns, z_half == 0)

    @pl.when(local_shapes)
    def _():
        shapes_in[...] = shapes_out[...]

    for j in (1, 3, 2):
        a_wait_last(0, j)
        last_near(j)
    c_pass()
    for q in (PLANE_AT[1], PLANE_AT[7]):
        a_wait_first(q, 0)
        v_send(q)
    for n, (dz, step) in enumerate(((2, -1), (6, 1))):
        q = PLANE_AT[dz]
        a_wait_first(q, 0)
        z_send(4 + 2 * n, q, PLANE_AT[(dz - step) % 8], step)
        z_send(5 + 2 * n, q, PLANE_AT[4], 2 * step, n)
        v_send(q)
    last_far(0)
    wait(c_flat.at[pl.ds(48, 144)], c2_rs)
    owner_row = owner_ref[...]
    r32 = lax.broadcasted_iota(i32, (32, 32), 0)
    c32 = lax.broadcasted_iota(i32, (32, 32), 1)
    owners = jnp.broadcast_to(owner_row, (32, 32))
    owner_col = jnp.sum(jnp.where(r32 == c32, owners, 0), axis=1, keepdims=True)
    rank = jnp.sum(
        jnp.logical_and(owners == owner_col, c32 < r32).astype(i32), axis=1, keepdims=True
    )
    slot = lax.broadcasted_iota(i32, (32, 64), 1)
    region_x = lax.rem(x + lax.rem(lax.div(slot, 2), 4), 4)
    region_y = lax.rem(y + lax.div(slot, 16), 4)
    region_c = lax.rem(core + lax.rem(slot, 2), 2)
    region = (region_x * 4 + region_y) * 2 + region_c
    chosen = jnp.logical_and(region == owner_col, lax.rem(lax.div(slot, 8), 2) == rank)
    chosen = chosen.astype(f32).astype(bf16)
    flat = jnp.concatenate(
        [
            jnp.concatenate(
                [c_flat[e * 48 + t * 16 : e * 48 + t * 16 + 16, :] for e in range(4)], axis=0
            )
            for t in range(3)
        ],
        axis=1,
    )
    high = flat.astype(bf16)
    low = (flat - high.astype(f32)).astype(bf16)
    high = jnp.dot(chosen, high, preferred_element_type=f32)
    low = jnp.dot(chosen, low, preferred_element_type=f32)
    hot_mine[...] = jnp.concatenate(
        [high[:, 0:256], high[:, 256:384] + swap(low[:, 256:384]), low[:, 0:256]], axis=1
    ).astype(bf16)
    hot_in[core] = hot_mine[...]
    for du in (2, 1, 3):
        for cc in range(2):
            here_u, here_v = (x, y) if cc == 0 else (y, x)
            copies.append(
                send(
                    hot_mine, hot_in.at[du * 2 + core], hot_ss.at[du * 2 + cc],
                    hot_rs.at[du * 2 + core], line(cc, lax.rem(here_u + 4 - du, 4), here_v, z, cc),
                )
            )
    copies.append(
        send(hot_mine, hot_in.at[core], hot_ss.at[0], hot_rs.at[core], at(x, y, z, 1 - core))
    )


    for q in (PLANE_AT[3], PLANE_AT[5]):
        a_wait_first(q, 0)
        v_send(q)
    for n in range(2):
        part = pl.ds(n * (SPLIT // 2), SPLIT // 2)
        wait(gathered.at[PLANE_AT[4] * 4, part], far_rs.at[n])
    v_send(PLANE_AT[4])
    for j in (1, 3, 2):
        last_far(j)
    @pl.when(jnp.logical_not(local_shapes))
    def _():
        wait(shapes_in, shp_rs)

    pad_shapes[0:304, :] = shapes_in[...].astype(f32)
    pad_shapes[304:384, :] = jnp.zeros((80, E_DEV), f32)
    shapes_t[...] = pad_shapes[...].T.astype(bf16)
    e_acc[...] = jnp.zeros_like(e_acc)

    def unfold(q):
        parts = []
        for pair in range(2):
            even = gathered[q * 4 + 2 * pair].astype(f32)
            odd = gathered[q * 4 + 2 * pair + 1].astype(f32)
            parts.append(
                (
                    jnp.where(left, even, swap(odd)).astype(bf16),
                    jnp.where(left, swap(even), odd).astype(bf16),
                )
            )
        first = jnp.concatenate([parts[0][0], parts[1][0]], axis=1)
        last = jnp.concatenate([parts[0][1], parts[1][1]], axis=1)
        wide[q, 0:160, :] = first
        wide[q, 160:320, :] = last
        wide[q, 320:384, :] = last[96:160]
        wide[q, 384:544, :] = first
        wide[q, 544:640, :] = last[0:96]

    def energies(q):
        stress = jnp.dot(shapes_t[...], wide[q, 0:384, :], preferred_element_type=f32)
        squares = stress * stress
        e_acc[...] += squares[:, 0:128] + squares[:, 128:256]

    def series(q):
        out = jnp.dot(
            hot_in[...].reshape(256, 640), wide[q], preferred_element_type=f32
        ).reshape(8, 2, 16, 256)
        for pair in range(2):
            lanes = slice(pair * 128, pair * 128 + 128)
            top = out[:, 0, :, lanes].reshape(128, 128)
            low_half = out[:, 1, :, lanes].reshape(128, 128)
            for n, tile in enumerate(
                (
                    jnp.where(left, top, swap(low_half)),
                    jnp.where(left, swap(top), low_half),
                )
            ):
                folded[pl.ds((q % 4) * 4 + pair * 2 + n, 128, stride=16), :] = tile

    def s_send(piece):
        sending[piece] = folded[...].astype(bf16).reshape(8, 16, 16, 128)
        arrived[core, 0, piece] = sending[piece, core]
        for du in (2, 1, 3):
            for cc in range(2):
                n = du * 2 + cc
                copies.append(
                    send(
                        sending.at[piece, n], arrived.at[core, (4 - du) % 4, piece],
                        s_ss.at[piece, n], s_rs.at[core, (4 - du) % 4, piece],
                        line(core, lax.rem(u + du, 4), v, z, cc),
                    )
                )
        copies.append(
            send(
                sending.at[piece, 1 - core], arrived.at[core, 0, piece], s_ss.at[piece, 0],
                s_rs.at[core, 0, piece], at(x, y, z, 1 - core),
            )
        )

    def planes(piece):
        for q in range(4 * piece, 4 * piece + 4):
            for j in range(4):
                if j:
                    a_wait_first(q, j)
                if q not in (PLANE_AT[0], PLANE_AT[2], PLANE_AT[6]):
                    a_wait_last(q, j)
            unfold(q)
            energies(q)

    planes(0)
    for du in range(1, 4):
        for cc in range(2):
            wait(hot_in.at[du * 2 + cc], hot_rs.at[du * 2 + cc])
    wait(hot_in.at[1 - core], hot_rs.at[1 - core])

    for q in range(4):
        series(q)
    s_send(0)
    planes(1)

    e_mine[0] = jnp.sum(e_acc[...].T, axis=0, keepdims=True)
    e_local = jnp.logical_and(z_half == 0, core == z_odd)
    e_to = line(core, lax.rem(u + z_half, 4), v, z, z_odd)

    def e_first(act):
        @pl.when(jnp.logical_not(e_local))
        def _():
            act(
                pltpu.make_async_remote_copy(
                    src_ref=e_mine, dst_ref=e_in.at[pl.ds(core, 1)], send_sem=e1_ss,
                    recv_sem=e1_rs.at[core], device_id=e_to, device_id_type=MESH,
                )
            )

    e_first(lambda copy: copy.start())

    @pl.when(e_local)
    def _():
        e_in[core] = e_mine[0]

    def a_wait(piece):
        for half in range(2):
            for du in range(1, 4):
                wait(arrived.at[half, du, piece], s_rs.at[half, du, piece])
        wait(arrived.at[1 - core, 0, piece], s_rs.at[1 - core, 0, piece])

    for q in range(4, 8):
        series(q)
    s_send(1)

    def e_slot(d):
        return lax.div(lax.rem(z + d, 8), 2)

    def e_wait(d):
        wait(e_all.at[pl.ds(e_slot(d), 1)], e2_rs.at[e_slot(d)])

    def e_copy(src, d, to, n):
        return pltpu.make_async_remote_copy(
            src_ref=src, dst_ref=e_all.at[pl.ds(e_slot(d), 1)], send_sem=e2_ss.at[n],
            recv_sem=e2_rs.at[e_slot(d)], device_id=at(x, y, lax.rem(z + to, 8), core),
            device_id_type=MESH,
        )

    def e_second(act):
        @pl.when(owns)
        def _():
            for n, to in enumerate((1, 7, 2, 6)):
                act(e_copy(e_sum, 0, to, n))

    def e_third(act):
        @pl.when(owns)
        def _():
            act(e_copy(e_all.at[pl.ds(e_slot(2), 1)], 2, 6, 4))

        @pl.when(jnp.logical_not(owns))
        def _():
            act(e_copy(e_all.at[pl.ds(e_slot(1), 1)], 1, 6, 4))
            act(e_copy(e_all.at[pl.ds(e_slot(7), 1)], 7, 2, 5))

    lax.fori_loop(0, 10, member_block, 0)

    @pl.when(owns)
    def _():
        for cc in range(2):

            @pl.when(jnp.logical_not(jnp.logical_and(z_half == 0, core == cc)))
            def _():
                wait(e_in.at[pl.ds(cc, 1)], e1_rs.at[cc])

        e_sum[0] = e_in[0] + e_in[1]
        e_all[z_half] = e_sum[0]

    e_second(lambda copy: copy.start())
    lax.fori_loop(10, 32, member_block, 0)
    a_wait(0)
    @pl.when(owns)
    def _():
        e_wait(2)

    @pl.when(jnp.logical_not(owns))
    def _():
        e_wait(1)
        e_wait(7)

    e_third(lambda copy: copy.start())

    a_wait(1)
    for pp in range(8):
        ones = []
        for half in range(2):
            tiles = []
            for n in range(2):
                tiles.append(
                    jnp.concatenate(
                        [
                            arrived[half, i, piece, 2 * pp + n]
                            for i in range(4)
                            for piece in range(2)
                        ],
                        axis=0,
                    )
                )
            ones.append(
                jnp.dot(table[half], jnp.concatenate(tiles, axis=1), preferred_element_type=f32)
            )
        for n in range(2):
            lanes = slice(n * 128, n * 128 + 128)
            for half in range(2):
                real, imag = ones[half][0:128, lanes], ones[half][128:256, lanes]
                c, s = turn_ref[2 * half], turn_ref[2 * half + 1]
                rows = slice((2 * pp + n) * 128, (2 * pp + n) * 128 + 128)
                twiddled[rows, half * 256 : half * 256 + 128] = (real * c + imag * s).astype(bf16)
                twiddled[rows, half * 256 + 128 : half * 256 + 256] = (
                    imag * c - real * s
                ).astype(bf16)

    second = second_ref[...].astype(bf16)
    for chunk in range(4):
        out = jnp.dot(
            twiddled[chunk * 512 : chunk * 512 + 512, :], second, preferred_element_type=f32
        )
        real, imag = out[:, 0:128], out[:, 128:256]
        squares = real * real + imag * imag
        for n in range(4):
            power[pl.ds(4 * chunk + n, 128, stride=16), :] = squares[n * 128 : n * 128 + 128]

    sums = jnp.zeros((HS_DEV, NB), f32)
    for kb in range(32):
        tiles = []
        for pair in range(2):
            base = (kb * 4 + pair * 2) * 16
            even, odd = power[base : base + 16, :], power[base + 16 : base + 32, :]
            tiles.append(
                jnp.concatenate(
                    [jnp.where(left, even, swap(odd)), jnp.where(left, swap(even), odd)], axis=0
                )
            )
        sums = sums + jnp.dot(
            jnp.concatenate(tiles, axis=1).astype(bf16),
            member[kb * 256 : kb * 256 + 256, :],
            preferred_element_type=f32,
        )
    band_ref[...] = sums / (NT * bins)

    @pl.when(owns)
    def _():
        e_wait(6)
        e_wait(4)

    @pl.when(jnp.logical_not(owns))
    def _():
        e_wait(3)
        e_wait(5)

    energy_ref[...] = jnp.sqrt(((e_all[0] + e_all[1]) + (e_all[2] + e_all[3])) / NT + epsilon).reshape(E_DEV)

    for copy in copies:
        copy.wait_send()
    wait(c_out.at[pl.ds(24, 168)], c1_ss)
    wait(c_next.at[pl.ds(48, 144)], c2_ss)
    shape_copies(lambda copy: copy.wait_send())
    e_first(lambda copy: copy.wait_send())
    e_second(lambda copy: copy.wait_send())
    e_third(lambda copy: copy.wait_send())


def shards(mode_record, mode_shapes, map_elem, map_coef, hot_owner, band_bins):
    f32, bf16 = jnp.float32, jnp.bfloat16
    first, turn, second = tables()
    vmem, dma = pltpu.VMEM, pltpu.SemaphoreType.DMA
    scratch = [
        vmem((HALF, MODES), bf16),
        vmem((MODES, E_DEV), bf16),
        vmem(map_elem.shape, jnp.int32),
        vmem(map_coef.shape, f32),
        vmem((1, HS_DEV), jnp.int32),
        vmem((1, NB), jnp.int32),
        vmem(first.shape, bf16),
        vmem(turn.shape, f32),
        vmem(second.shape, f32),
        vmem((128, 384), f32),
        vmem((384, 384), f32),
        vmem((304, 384), bf16),
        vmem((304, 384), bf16),
        vmem((384, 384), bf16),
        vmem((384, 128), f32),
        vmem((192, 128), f32),
        vmem((192, 128), f32),
        vmem((192, 128), f32),
        vmem((192, 128), f32),
        vmem((32, 640), bf16),
        vmem((8, 32, 640), bf16),
        vmem((32, FOLD, 128), bf16),
        vmem((8, 640, 256), bf16),
        vmem((2048, 128), f32),
        vmem((2, 8, 16, 16, 128), bf16),
        vmem((2, 4, 2, 16, 16, 128), bf16),
        vmem((NT // 2, NB), bf16),
        vmem((2048, 512), bf16),
        vmem((2048, 128), f32),
        vmem((2, 256, 128), bf16),
        vmem((384, 128), f32),
        vmem((1, 1, 384), f32),
        vmem((2, 1, 384), f32),
        vmem((1, 1, 384), f32),
        vmem((4, 1, 384), f32),
        dma((2,)), dma, dma, dma, dma, dma, dma((8,)), dma((8,)), dma((24,)), dma((32,)), dma((8,)), dma((2,)), dma((31,)), dma((32,)),
        dma((2, 8)), dma((2, 4, 2)), dma, dma((2,)), dma((8,)), dma((4,)),
        dma((9,)),
    ]
    whole = pl.BlockSpec(memory_space=pltpu.VMEM)
    sums, energy = pl.pallas_call(
        kernel,
        out_shape=(
            pltpu.VMEM((HS_DEV, NB), f32),
            pltpu.VMEM((E_DEV,), f32),
        ),
        in_specs=[pl.BlockSpec(memory_space=pltpu.HBM)] * 9,
        out_specs=(whole, whole),
        scratch_shapes=scratch,
        compiler_params=pltpu.CompilerParams(
            collective_id=0, has_side_effects=True, vmem_limit_bytes=255 * 2**18
        ),
        name="whipping",
    )(
        mode_record.T, mode_shapes, map_elem, map_coef, hot_owner.reshape(1, HS_DEV),
        band_bins.reshape(1, NB), jnp.asarray(first), jnp.asarray(turn), jnp.asarray(second),
    )
    return (energy, sums)


def solution(mesh):
    in_specs = (
        P(None, ("ta", "ha")),
        P(None, "ha"),
        P(None, "ha"),
        P(None, "ha"),
        P(("ta", "ha")),
        P(),
    )
    out_specs = (P("ha"), P(("ta", "ha"), None))
    return jax.shard_map(shards, mesh=mesh, in_specs=in_specs, out_specs=out_specs, check_vma=False)
```

```python
import jax
import jax.numpy as jnp
import numpy as np
from jax import lax
from jax.experimental import pallas as pl
from jax.experimental.pallas import tpu as pltpu
from jax.sharding import PartitionSpec as P

DFT_LEN = 128
NB = 512
K_EXT = 4
HS_DEV = 32
NT = 16384
MODES = 300
E_DEV = 384
FOLD = 160
SPLIT = 96
KPAD = 320
HALF = 64

epsilon = 1e-06
MESH = pl.DeviceIdType.MESH
PLANES = (0, 1, 7, 2, 6, 3, 5, 4)
PLANE_AT = {dz: i for i, dz in enumerate(PLANES)}


def tables():
    import ml_dtypes

    pos = np.arange(DFT_LEN)
    turn = np.float32(2.0 * np.pi / DFT_LEN)
    first = (pos[:, None] * pos[None, :] % DFT_LEN).astype(np.float32) * turn
    first_table = np.concatenate([np.cos(first), -np.sin(first)], axis=0)
    fine = (pos[:, None] * pos[None, :]).astype(np.float32) * np.float32(2.0 * np.pi / NT)
    twiddle = []
    for half in range(2):
        part = fine[:, half * HALF : (half + 1) * HALF]
        part = np.concatenate([part, part], axis=1)
        twiddle += [np.cos(part), np.sin(part)]
    second = np.zeros((4, 2, HALF, 2, 2, HALF), np.float32)
    for half in range(2):
        angles = first[half * HALF : (half + 1) * HALF, :HALF]
        c, s = np.cos(angles), np.sin(angles)
        for hh in range(2):
            second[2 * half, hh, :, 0, hh] = c
            second[2 * half, hh, :, 1, hh] = -s
            second[2 * half + 1, hh, :, 0, hh] = s
            second[2 * half + 1, hh, :, 1, hh] = c
    return (
        first_table.astype(ml_dtypes.bfloat16),
        np.stack(twiddle).astype(np.float32),
        second.reshape(512, 256).astype(ml_dtypes.bfloat16).astype(np.float32),
    )


def kernel(
    rec_hbm, shapes_hbm, elem_hbm, coef_hbm, owner_hbm, bins_hbm, first_hbm, turn_hbm, second_hbm,
    band_ref, energy_ref,
    rec_ref, shapes_ref, elem_ref, coef_ref, owner_ref, bins_ref, first_ref, turn_ref, second_ref,
    pad_rec, pad_shapes, shapes_out, shapes_in, shapes_t,
    c_rows, c_out, c_mid, c_next, c_flat, hot_mine, hot_in,
    gathered, wide, folded, sending, arrived,
    member, twiddled, power, table, e_acc, e_mine, e_in, e_sum, e_all,
    shp_ss, shp_rs, c1_ss, c1_rs, c2_ss, c2_rs, hot_ss, hot_rs, g_ss, g_rs, z_ss, far_rs, h_ss, h_rs, s_ss, s_rs, e1_ss, e1_rs, e2_ss, e2_rs,
    in_sem,
):
    f32, bf16, i32 = jnp.float32, jnp.bfloat16, jnp.int32
    z = lax.axis_index("ta")
    ha = lax.axis_index("ha")
    core = lax.rem(ha, 2)
    x = lax.div(ha, 8)
    y = lax.rem(lax.div(ha, 2), 4)
    u = jnp.where(core == 0, x, y)
    v = jnp.where(core == 0, y, x)
    z_half, z_odd = lax.div(z, 2), lax.rem(z, 2)

    def at(px, py, pz, pc):
        return (pz, (px * 4 + py) * 2 + pc)

    def line(plane_core, pu, pv, pz, pc):
        return at(
            jnp.where(plane_core == 0, pu, pv), jnp.where(plane_core == 0, pv, pu), pz, pc
        )

    def send(src, dst, ss, rs, device):
        copy = pltpu.make_async_remote_copy(
            src_ref=src, dst_ref=dst, send_sem=ss, recv_sem=rs, device_id=device, device_id_type=MESH
        )
        copy.start()
        return copy

    def wait(ref, sem):
        pltpu.make_async_copy(ref, ref, sem).wait()

    fetches = [
        pltpu.make_async_copy(src, dst, in_sem.at[n])
        for n, (src, dst) in enumerate(
            (
                (rec_hbm, rec_ref), (shapes_hbm, shapes_ref), (elem_hbm, elem_ref),
                (coef_hbm, coef_ref), (first_hbm, first_ref), (bins_hbm, bins_ref),
                (owner_hbm, owner_ref), (second_hbm, second_ref), (turn_hbm, turn_ref),
            )
        )
    ]
    for fetch in fetches:
        fetch.start()

    barrier = pltpu.get_barrier_semaphore()

    partners = [at(x, y, lax.rem(z + dz, 8), core) for dz in (1, 7, 2, 6)]
    for d in (1, 3, 2):
        for pc in range(2):
            partners.append(at(x, lax.rem(y + d, 4), z, pc))
            partners.append(at(lax.rem(x + d, 4), y, z, pc))
    partners.append(at(x, y, z, 1 - core))
    for partner in partners:
        pl.semaphore_signal(barrier, inc=1, device_id=partner, device_id_type=MESH)

    lane128 = lax.broadcasted_iota(i32, (1, 128), 1)
    left = lane128 < HALF

    def swap(tile):
        return pltpu.roll(tile, HALF, 1)

    pad_rec[...] = jnp.zeros_like(pad_rec)
    fetches[0].wait()
    pad_rec[0:HALF, 0:MODES] = rec_ref[...].astype(f32)
    turned = pad_rec[...].T
    gathered[0] = (turned[0:FOLD] + swap(turned[FOLD : 2 * FOLD])).astype(bf16)

    shapes_out[MODES - 12 : 304, :] = jnp.zeros((16, E_DEV), bf16)
    for fetch in fetches[1:4]:
        fetch.wait()
    shapes_out[0:MODES, :] = shapes_ref[...]
    slots = pl.ds(pl.multiple_of(z_half * 128, 128), 128)
    elems = elem_ref[:, slots]
    coefs = coef_ref[:, slots]
    elem_ids = lax.broadcasted_iota(i32, (E_DEV, 128), 0)
    hot = jnp.zeros((304, 128), f32)
    for k in range(K_EXT):
        pick = (elem_ids == elems[k : k + 1, :]).astype(f32).astype(bf16)
        hot = hot + coefs[k : k + 1, :] * jnp.dot(
            shapes_out[...], pick, preferred_element_type=f32
        )
    hot = jnp.concatenate([hot, jnp.zeros((80, 128), f32)], axis=0).T
    for t in range(3):
        c_rows[t * 128 : t * 128 + 128, :] = hot[:, t * 128 : t * 128 + 128]

    for g in range(8):
        for t in range(3):
            for rank in range(2):
                start = t * 128 + z_odd * HALF + 16 * (g // 2) + 2 * (g % 2) + rank
                to = (g * 3 + t) * 8 + rank * 4
                c_out[to : to + 4, :] = c_rows[pl.ds(start, 4, stride=4), :]

    col = lax.broadcasted_iota(i32, (128, 128), 1)
    row = lax.broadcasted_iota(i32, (128, 128), 0)
    source, place, dv = lax.div(col, 32), lax.div(lax.rem(col, 32), 4), lax.rem(col, 4)
    dz = jnp.zeros_like(col)
    for i, value in enumerate(PLANES):
        dz = jnp.where(place == i, value, dz)
    zz = lax.rem(z + dz, 8)
    a_even = 16 * zz + 4 * lax.rem(x + source, 4) + lax.rem(y + dv, 4)
    a_odd = 16 * zz + 4 * lax.rem(x + dv, 4) + lax.rem(y + source, 4)
    fetches[4].wait()
    for half, a_of in enumerate((a_even, a_odd)):
        order = (row == a_of).astype(f32).astype(bf16)
        table[half] = jnp.dot(first_ref[...], order, preferred_element_type=f32).astype(bf16)

    for fetch in fetches[5:]:
        fetch.wait()
    bins = bins_ref[...].astype(f32)
    before = (
        lax.broadcasted_iota(i32, (NB, NB), 0) < lax.broadcasted_iota(i32, (NB, NB), 1)
    ).astype(f32).astype(bf16)
    starts = jnp.dot(
        jnp.broadcast_to(bins, (8, NB)).astype(bf16), before, preferred_element_type=f32
    )[0:1]
    starts_i = starts.astype(i32)
    ends_i = (starts + bins).astype(i32)

    def member_block(i, _):
        rows = lax.broadcasted_iota(i32, (256, 1), 0)
        bin_ids = i * 4 + lax.div(rows, HALF) + DFT_LEN * lax.rem(rows, HALF)
        inside = jnp.logical_and(bin_ids >= starts_i, bin_ids < ends_i)
        member[pl.ds(pl.multiple_of(i * 256, 256), 256), :] = inside.astype(f32).astype(bf16)
        return 0

    owner_row = owner_ref[...]
    r32 = lax.broadcasted_iota(i32, (32, 32), 0)
    c32 = lax.broadcasted_iota(i32, (32, 32), 1)
    owners = jnp.broadcast_to(owner_row, (32, 32))
    owner_col = jnp.sum(jnp.where(r32 == c32, owners, 0), axis=1, keepdims=True)
    rank = jnp.sum(
        jnp.logical_and(owners == owner_col, c32 < r32).astype(i32), axis=1, keepdims=True
    )
    slot = lax.broadcasted_iota(i32, (32, 64), 1)
    region_x = lax.rem(x + lax.rem(lax.div(slot, 2), 4), 4)
    region_y = lax.rem(y + lax.div(slot, 16), 4)
    region_c = lax.rem(core + lax.rem(slot, 2), 2)
    region = (region_x * 4 + region_y) * 2 + region_c
    chosen = jnp.logical_and(region == owner_col, lax.rem(lax.div(slot, 8), 2) == rank)
    chosen = chosen.astype(f32).astype(bf16)
    pl.semaphore_wait(barrier, len(partners))

    copies = []

    first_rows, last_rows = pl.ds(0, SPLIT), pl.ds(SPLIT, FOLD - SPLIT)

    def a_wait_first(q, j):
        wait(gathered.at[q * 4 + j, first_rows], g_rs.at[q * 4 + j])

    def a_wait_last(q, j):
        wait(gathered.at[q * 4 + j, last_rows], h_rs.at[q * 4 + j])

    def v_send(q):
        for j in (2, 1, 3):
            copies.append(
                send(
                    gathered.at[q * 4, first_rows], gathered.at[q * 4 + j, first_rows],
                    g_ss.at[3 * q + j - 1], g_rs.at[q * 4 + j],
                    line(core, u, lax.rem(v + 4 - j, 4), z, core),
                )
            )

    def z_send(n, q, dq, dz, rows=None):
        src, dst = gathered.at[q * 4, first_rows], gathered.at[dq * 4, first_rows]
        rs = g_rs.at[dq * 4]
        if rows is not None:
            part = pl.ds(rows * (SPLIT // 2), SPLIT // 2)
            src, dst, rs = gathered.at[q * 4, part], gathered.at[dq * 4, part], far_rs.at[rows]
        copies.append(send(src, dst, z_ss.at[n], rs, at(x, y, lax.rem(z + 8 + dz, 8), core)))

    def last_v_send():
        for j in (2, 1, 3):
            copies.append(
                send(
                    gathered.at[0, last_rows], gathered.at[j, last_rows], h_ss.at[j - 1],
                    h_rs.at[j], line(core, u, lax.rem(v + 4 - j, 4), z, core),
                )
            )

    last_count = [3]

    def last_z_send(dz, to, j):
        q, dq = PLANE_AT[dz % 8], PLANE_AT[(dz - to) % 8]
        n = last_count[0]
        last_count[0] += 1
        copies.append(
            send(
                gathered.at[q * 4 + j, last_rows], gathered.at[dq * 4 + j, last_rows], h_ss.at[n],
                h_rs.at[dq * 4 + j], at(x, y, lax.rem(z + 8 + to, 8), core),
            )
        )

    def last_near(j):
        for to in (1, -1, 2, -2):
            last_z_send(0, to, j)

    def last_far(j):
        a_wait_last(PLANE_AT[2], j)
        last_z_send(2, -1, j)
        if j in (0, 1):
            last_z_send(2, -2, j)
        a_wait_last(PLANE_AT[6], j)
        last_z_send(-2, 1, j)
        if j in (2, 3):
            last_z_send(-2, 2, j)

    def group(px, pc):
        return pl.ds(pl.multiple_of(24 * (px * 2 + pc), 8), 24)

    for dx in (2, 1, 3, 0):
        for dc in range(2):
            to_x, to_c = lax.rem(x + dx, 4), jnp.where(dc == 0, core, 1 - core)
            if dx or dc:
                g = ((4 - dx) % 4) * 2 + dc
                send(
                    c_out.at[group(to_x, to_c)], c_mid.at[pl.ds(24 * g, 24)], c1_ss, c1_rs,
                    at(to_x, y, z, to_c),
                )
    c_mid[0:24, :] = c_out[group(x, core), :]

    for n, dz in enumerate((1, 7, 2, 6)):
        z_send(n, 0, PLANE_AT[dz], -dz)
    last_v_send()
    last_near(0)
    v_send(0)

    def c_pass():
        wait(c_mid.at[pl.ds(24, 168)], c1_rs)
        for dy in (2, 1, 3, 0):
            to_y = lax.rem(y + dy, 4)
            for t in range(3):
                for rank in range(2):
                    to = dy * 48 + t * 16 + rank * 8
                    c_next[to : to + 8, :] = c_mid[
                        pl.ds(t * 8 + rank * 4 + to_y, 8, stride=24), :
                    ]
            if dy:
                send(
                    c_next.at[pl.ds(dy * 48, 48)], c_flat.at[pl.ds((4 - dy) * 48, 48)], c2_ss,
                    c2_rs, at(x, to_y, z, core),
                )
        c_flat[0:48, :] = c_next[0:48, :]

    owns = core == z_odd
    shp_to = [
        line(0, lax.rem(x + 4 - z_half, 4), y, z, 0),
        line(1, lax.rem(y + 4 - z_half, 4), x, z, 1),
    ]

    def shape_copies(act):
        for cc in range(2):
            own_work = jnp.logical_and(z_half == 0, core == cc)

            @pl.when(jnp.logical_and(owns, jnp.logical_not(own_work)))
            def _():
                act(
                    pltpu.make_async_remote_copy(
                        src_ref=shapes_out, dst_ref=shapes_in, send_sem=shp_ss.at[cc],
                        recv_sem=shp_rs, device_id=shp_to[cc], device_id_type=MESH,
                    )
                )

    shape_copies(lambda copy: copy.start())
    local_shapes = jnp.logical_and(owns, z_half == 0)

    @pl.when(local_shapes)
    def _():
        shapes_in[...] = shapes_out[...]

    for j in (1, 3, 2):
        a_wait_last(0, j)
        last_near(j)
    c_pass()
    for q in (PLANE_AT[1], PLANE_AT[7]):
        a_wait_first(q, 0)
        v_send(q)
    for n, (dz, step) in enumerate(((2, -1), (6, 1))):
        q = PLANE_AT[dz]
        a_wait_first(q, 0)
        z_send(4 + 2 * n, q, PLANE_AT[(dz - step) % 8], step)
        z_send(5 + 2 * n, q, PLANE_AT[4], 2 * step, n)
        v_send(q)
    last_far(0)
    wait(c_flat.at[pl.ds(48, 144)], c2_rs)
    flat = jnp.concatenate(
        [
            jnp.concatenate(
                [c_flat[e * 48 + t * 16 : e * 48 + t * 16 + 16, :] for e in range(4)], axis=0
            )
            for t in range(3)
        ],
        axis=1,
    )
    high = flat.astype(bf16)
    low = (flat - high.astype(f32)).astype(bf16)
    both = jnp.dot(
        chosen, jnp.concatenate([high, low], axis=1), preferred_element_type=f32
    )
    high, low = both[:, 0:384], both[:, 384:768]
    hot_mine[...] = jnp.concatenate(
        [high[:, 0:256], high[:, 256:384] + swap(low[:, 256:384]), low[:, 0:256]], axis=1
    ).astype(bf16)
    for du in (2, 1, 3):
        for cc in range(2):
            here_u, here_v = (x, y) if cc == 0 else (y, x)
            copies.append(
                send(
                    hot_mine, hot_in.at[du * 2 + core], hot_ss.at[du * 2 + cc],
                    hot_rs.at[du * 2 + core], line(cc, lax.rem(here_u + 4 - du, 4), here_v, z, cc),
                )
            )
    copies.append(
        send(hot_mine, hot_in.at[core], hot_ss.at[0], hot_rs.at[core], at(x, y, z, 1 - core))
    )
    hot_in[core] = hot_mine[...]


    for q in (PLANE_AT[3], PLANE_AT[5]):
        a_wait_first(q, 0)
        v_send(q)
    for n in range(2):
        part = pl.ds(n * (SPLIT // 2), SPLIT // 2)
        wait(gathered.at[PLANE_AT[4] * 4, part], far_rs.at[n])
    v_send(PLANE_AT[4])
    for j in (1, 3, 2):
        last_far(j)
    @pl.when(jnp.logical_not(local_shapes))
    def _():
        wait(shapes_in, shp_rs)

    pad_shapes[0:304, :] = shapes_in[...].astype(f32)
    pad_shapes[304:384, :] = jnp.zeros((80, E_DEV), f32)
    shapes_t[...] = pad_shapes[...].T.astype(bf16)
    e_acc[...] = jnp.zeros_like(e_acc)

    def unfold(q):
        parts = []
        for pair in range(2):
            even = gathered[q * 4 + 2 * pair].astype(f32)
            odd = gathered[q * 4 + 2 * pair + 1].astype(f32)
            parts.append(
                (
                    jnp.where(left, even, swap(odd)).astype(bf16),
                    jnp.where(left, swap(even), odd).astype(bf16),
                )
            )
        first = jnp.concatenate([parts[0][0], parts[1][0]], axis=1)
        last = jnp.concatenate([parts[0][1], parts[1][1]], axis=1)
        wide[q, 0:160, :] = first
        wide[q, 160:320, :] = last
        wide[q, 320:384, :] = last[96:160]
        wide[q, 384:544, :] = first
        wide[q, 544:640, :] = last[0:96]

    def energies(q):
        stress = jnp.dot(shapes_t[...], wide[q, 0:384, :], preferred_element_type=f32)
        squares = stress * stress
        e_acc[...] += squares[:, 0:128] + squares[:, 128:256]

    def series(q):
        out = jnp.dot(
            hot_in[...].reshape(256, 640), wide[q], preferred_element_type=f32
        ).reshape(8, 2, 16, 256)
        for pair in range(2):
            lanes = slice(pair * 128, pair * 128 + 128)
            top = out[:, 0, :, lanes].reshape(128, 128)
            low_half = out[:, 1, :, lanes].reshape(128, 128)
            for n, tile in enumerate(
                (
                    jnp.where(left, top, swap(low_half)),
                    jnp.where(left, swap(top), low_half),
                )
            ):
                folded[pl.ds((q % 4) * 4 + pair * 2 + n, 128, stride=16), :] = tile

    def s_send(piece):
        sending[piece] = folded[...].astype(bf16).reshape(8, 16, 16, 128)
        arrived[core, 0, piece] = sending[piece, core]
        for du in (2, 1, 3):
            for cc in range(2):
                n = du * 2 + cc
                copies.append(
                    send(
                        sending.at[piece, n], arrived.at[core, (4 - du) % 4, piece],
                        s_ss.at[piece, n], s_rs.at[core, (4 - du) % 4, piece],
                        line(core, lax.rem(u + du, 4), v, z, cc),
                    )
                )
        copies.append(
            send(
                sending.at[piece, 1 - core], arrived.at[core, 0, piece], s_ss.at[piece, 0],
                s_rs.at[core, 0, piece], at(x, y, z, 1 - core),
            )
        )

    def planes(piece):
        for q in range(4 * piece, 4 * piece + 4):
            for j in range(4):
                if j:
                    a_wait_first(q, j)
                if q not in (PLANE_AT[0], PLANE_AT[2], PLANE_AT[6]):
                    a_wait_last(q, j)
            unfold(q)
            energies(q)

    planes(0)
    for du in range(1, 4):
        for cc in range(2):
            wait(hot_in.at[du * 2 + cc], hot_rs.at[du * 2 + cc])
    wait(hot_in.at[1 - core], hot_rs.at[1 - core])

    for q in range(4):
        series(q)
    s_send(0)
    planes(1)

    e_mine[0] = jnp.sum(e_acc[...].T, axis=0, keepdims=True)
    e_local = jnp.logical_and(z_half == 0, core == z_odd)
    e_to = line(core, lax.rem(u + z_half, 4), v, z, z_odd)

    def e_first(act):
        @pl.when(jnp.logical_not(e_local))
        def _():
            act(
                pltpu.make_async_remote_copy(
                    src_ref=e_mine, dst_ref=e_in.at[pl.ds(core, 1)], send_sem=e1_ss,
                    recv_sem=e1_rs.at[core], device_id=e_to, device_id_type=MESH,
                )
            )

    e_first(lambda copy: copy.start())

    @pl.when(e_local)
    def _():
        e_in[core] = e_mine[0]

    def a_wait(piece):
        for half in range(2):
            for du in range(1, 4):
                wait(arrived.at[half, du, piece], s_rs.at[half, du, piece])
        wait(arrived.at[1 - core, 0, piece], s_rs.at[1 - core, 0, piece])

    for q in range(4, 8):
        series(q)
    s_send(1)

    def e_slot(d):
        return lax.div(lax.rem(z + d, 8), 2)

    def e_wait(d):
        wait(e_all.at[pl.ds(e_slot(d), 1)], e2_rs.at[e_slot(d)])

    def e_copy(src, d, to, n):
        return pltpu.make_async_remote_copy(
            src_ref=src, dst_ref=e_all.at[pl.ds(e_slot(d), 1)], send_sem=e2_ss.at[n],
            recv_sem=e2_rs.at[e_slot(d)], device_id=at(x, y, lax.rem(z + to, 8), core),
            device_id_type=MESH,
        )

    def e_second(act):
        @pl.when(owns)
        def _():
            for n, to in enumerate((1, 7, 2, 6)):
                act(e_copy(e_sum, 0, to, n))

    def e_third(act):
        @pl.when(owns)
        def _():
            act(e_copy(e_all.at[pl.ds(e_slot(2), 1)], 2, 6, 4))

        @pl.when(jnp.logical_not(owns))
        def _():
            act(e_copy(e_all.at[pl.ds(e_slot(1), 1)], 1, 6, 4))
            act(e_copy(e_all.at[pl.ds(e_slot(7), 1)], 7, 2, 5))

    lax.fori_loop(0, 10, member_block, 0)

    @pl.when(owns)
    def _():
        for cc in range(2):

            @pl.when(jnp.logical_not(jnp.logical_and(z_half == 0, core == cc)))
            def _():
                wait(e_in.at[pl.ds(cc, 1)], e1_rs.at[cc])

        e_sum[0] = e_in[0] + e_in[1]
        e_all[z_half] = e_sum[0]

    e_second(lambda copy: copy.start())
    lax.fori_loop(10, 32, member_block, 0)
    a_wait(0)
    @pl.when(owns)
    def _():
        e_wait(2)

    @pl.when(jnp.logical_not(owns))
    def _():
        e_wait(1)
        e_wait(7)

    e_third(lambda copy: copy.start())

    a_wait(1)
    for pp in range(8):
        ones = []
        for half in range(2):
            tiles = []
            for n in range(2):
                tiles.append(
                    jnp.concatenate(
                        [
                            arrived[half, i, piece, 2 * pp + n]
                            for i in range(4)
                            for piece in range(2)
                        ],
                        axis=0,
                    )
                )
            ones.append(
                jnp.dot(table[half], jnp.concatenate(tiles, axis=1), preferred_element_type=f32)
            )
        for n in range(2):
            lanes = slice(n * 128, n * 128 + 128)
            for half in range(2):
                real, imag = ones[half][0:128, lanes], ones[half][128:256, lanes]
                c, s = turn_ref[2 * half], turn_ref[2 * half + 1]
                rows = slice((2 * pp + n) * 128, (2 * pp + n) * 128 + 128)
                twiddled[rows, half * 256 : half * 256 + 128] = (real * c + imag * s).astype(bf16)
                twiddled[rows, half * 256 + 128 : half * 256 + 256] = (
                    imag * c - real * s
                ).astype(bf16)

    second = second_ref[...].astype(bf16)
    for chunk in range(4):
        out = jnp.dot(
            twiddled[chunk * 512 : chunk * 512 + 512, :], second, preferred_element_type=f32
        )
        real, imag = out[:, 0:128], out[:, 128:256]
        squares = real * real + imag * imag
        for n in range(4):
            power[pl.ds(4 * chunk + n, 128, stride=16), :] = squares[n * 128 : n * 128 + 128]

    sums = jnp.zeros((HS_DEV, NB), f32)
    for kb in range(32):
        tiles = []
        for pair in range(2):
            base = (kb * 4 + pair * 2) * 16
            even, odd = power[base : base + 16, :], power[base + 16 : base + 32, :]
            tiles.append(
                jnp.concatenate(
                    [jnp.where(left, even, swap(odd)), jnp.where(left, swap(even), odd)], axis=0
                )
            )
        sums = sums + jnp.dot(
            jnp.concatenate(tiles, axis=1).astype(bf16),
            member[kb * 256 : kb * 256 + 256, :],
            preferred_element_type=f32,
        )
    band_ref[...] = sums / (NT * bins)

    @pl.when(owns)
    def _():
        e_wait(6)
        e_wait(4)

    @pl.when(jnp.logical_not(owns))
    def _():
        e_wait(3)
        e_wait(5)

    energy_ref[...] = jnp.sqrt(((e_all[0] + e_all[1]) + (e_all[2] + e_all[3])) / NT + epsilon).reshape(E_DEV)

    for copy in copies:
        copy.wait_send()
    wait(c_out.at[pl.ds(24, 168)], c1_ss)
    wait(c_next.at[pl.ds(48, 144)], c2_ss)
    shape_copies(lambda copy: copy.wait_send())
    e_first(lambda copy: copy.wait_send())
    e_second(lambda copy: copy.wait_send())
    e_third(lambda copy: copy.wait_send())


def shards(mode_record, mode_shapes, map_elem, map_coef, hot_owner, band_bins):
    f32, bf16 = jnp.float32, jnp.bfloat16
    first, turn, second = tables()
    vmem, dma = pltpu.VMEM, pltpu.SemaphoreType.DMA
    scratch = [
        vmem((HALF, MODES), bf16),
        vmem((MODES, E_DEV), bf16),
        vmem(map_elem.shape, jnp.int32),
        vmem(map_coef.shape, f32),
        vmem((1, HS_DEV), jnp.int32),
        vmem((1, NB), jnp.int32),
        vmem(first.shape, bf16),
        vmem(turn.shape, f32),
        vmem(second.shape, f32),
        vmem((128, 384), f32),
        vmem((384, 384), f32),
        vmem((304, 384), bf16),
        vmem((304, 384), bf16),
        vmem((384, 384), bf16),
        vmem((384, 128), f32),
        vmem((192, 128), f32),
        vmem((192, 128), f32),
        vmem((192, 128), f32),
        vmem((192, 128), f32),
        vmem((32, 640), bf16),
        vmem((8, 32, 640), bf16),
        vmem((32, FOLD, 128), bf16),
        vmem((8, 640, 256), bf16),
        vmem((2048, 128), f32),
        vmem((2, 8, 16, 16, 128), bf16),
        vmem((2, 4, 2, 16, 16, 128), bf16),
        vmem((NT // 2, NB), bf16),
        vmem((2048, 512), bf16),
        vmem((2048, 128), f32),
        vmem((2, 256, 128), bf16),
        vmem((384, 128), f32),
        vmem((1, 1, 384), f32),
        vmem((2, 1, 384), f32),
        vmem((1, 1, 384), f32),
        vmem((4, 1, 384), f32),
        dma((2,)), dma, dma, dma, dma, dma, dma((8,)), dma((8,)), dma((24,)), dma((32,)), dma((8,)), dma((2,)), dma((31,)), dma((32,)),
        dma((2, 8)), dma((2, 4, 2)), dma, dma((2,)), dma((8,)), dma((4,)),
        dma((9,)),
    ]
    whole = pl.BlockSpec(memory_space=pltpu.VMEM)
    sums, energy = pl.pallas_call(
        kernel,
        out_shape=(
            pltpu.VMEM((HS_DEV, NB), f32),
            pltpu.VMEM((E_DEV,), f32),
        ),
        in_specs=[pl.BlockSpec(memory_space=pltpu.HBM)] * 9,
        out_specs=(whole, whole),
        scratch_shapes=scratch,
        compiler_params=pltpu.CompilerParams(
            collective_id=0, has_side_effects=True, vmem_limit_bytes=255 * 2**18
        ),
        name="whipping",
    )(
        mode_record.T, mode_shapes, map_elem, map_coef, hot_owner.reshape(1, HS_DEV),
        band_bins.reshape(1, NB), jnp.asarray(first), jnp.asarray(turn), jnp.asarray(second),
    )
    return (energy, sums)


def solution(mesh):
    in_specs = (
        P(None, ("ta", "ha")),
        P(None, "ha"),
        P(None, "ha"),
        P(None, "ha"),
        P(("ta", "ha")),
        P(),
    )
    out_specs = (P("ha"), P(("ta", "ha"), None))
    return jax.shard_map(shards, mesh=mesh, in_specs=in_specs, out_specs=out_specs, check_vma=False)
```

```python
import jax
import jax.numpy as jnp
import numpy as np
from jax import lax
from jax.experimental import pallas as pl
from jax.experimental.pallas import tpu as pltpu
from jax.sharding import PartitionSpec as P

DFT_LEN = 128
NB = 512
K_EXT = 4
HS_DEV = 32
NT = 16384
MODES = 300
E_DEV = 384
FOLD = 160
SPLIT = 96
KPAD = 320
HALF = 64

epsilon = 1e-06
MESH = pl.DeviceIdType.MESH
PLANES = (0, 1, 7, 2, 6, 3, 5, 4)
PLANE_AT = {dz: i for i, dz in enumerate(PLANES)}


def tables():
    import ml_dtypes

    pos = np.arange(DFT_LEN)
    turn = np.float32(2.0 * np.pi / DFT_LEN)
    first = (pos[:, None] * pos[None, :] % DFT_LEN).astype(np.float32) * turn
    first_table = np.concatenate([np.cos(first), -np.sin(first)], axis=0)
    fine = (pos[:, None] * pos[None, :]).astype(np.float32) * np.float32(2.0 * np.pi / NT)
    twiddle = []
    for half in range(2):
        part = fine[:, half * HALF : (half + 1) * HALF]
        part = np.concatenate([part, part], axis=1)
        twiddle += [np.cos(part), np.sin(part)]
    second = np.zeros((4, 2, HALF, 2, 2, HALF), np.float32)
    for half in range(2):
        angles = first[half * HALF : (half + 1) * HALF, :HALF]
        c, s = np.cos(angles), np.sin(angles)
        for hh in range(2):
            second[2 * half, hh, :, 0, hh] = c
            second[2 * half, hh, :, 1, hh] = -s
            second[2 * half + 1, hh, :, 0, hh] = s
            second[2 * half + 1, hh, :, 1, hh] = c
    return (
        first_table.astype(ml_dtypes.bfloat16),
        np.stack(twiddle).astype(np.float32),
        second.reshape(512, 256).astype(ml_dtypes.bfloat16).astype(np.float32),
    )


def kernel(
    rec_hbm, shapes_hbm, elem_hbm, coef_hbm, owner_hbm, bins_hbm, first_hbm, turn_hbm, second_hbm,
    band_ref, energy_ref,
    rec_ref, shapes_ref, elem_ref, coef_ref, owner_ref, bins_ref, first_ref, turn_ref, second_ref,
    pad_rec, pad_shapes, shapes_out, shapes_in, shapes_t,
    c_rows, c_out, c_mid, c_next, c_flat, hot_mine, hot_in,
    gathered, wide, folded, sending, arrived,
    member, twiddled, power, table, e_acc, e_mine, e_in, e_sum, e_all,
    shp_ss, shp_rs, c1_ss, c1_rs, c2_ss, c2_rs, hot_ss, hot_rs, g_ss, g_rs, z_ss, far_rs, h_ss, h_rs, s_ss, s_rs, e1_ss, e1_rs, e2_ss, e2_rs,
    in_sem,
):
    f32, bf16, i32 = jnp.float32, jnp.bfloat16, jnp.int32
    z = lax.axis_index("ta")
    ha = lax.axis_index("ha")
    core = lax.rem(ha, 2)
    x = lax.div(ha, 8)
    y = lax.rem(lax.div(ha, 2), 4)
    u = jnp.where(core == 0, x, y)
    v = jnp.where(core == 0, y, x)
    z_half, z_odd = lax.div(z, 2), lax.rem(z, 2)

    def at(px, py, pz, pc):
        return (pz, (px * 4 + py) * 2 + pc)

    def line(plane_core, pu, pv, pz, pc):
        return at(
            jnp.where(plane_core == 0, pu, pv), jnp.where(plane_core == 0, pv, pu), pz, pc
        )

    def send(src, dst, ss, rs, device):
        copy = pltpu.make_async_remote_copy(
            src_ref=src, dst_ref=dst, send_sem=ss, recv_sem=rs, device_id=device, device_id_type=MESH
        )
        copy.start()
        return copy

    def wait(ref, sem):
        pltpu.make_async_copy(ref, ref, sem).wait()

    fetches = [
        pltpu.make_async_copy(src, dst, in_sem.at[n])
        for n, (src, dst) in enumerate(
            (
                (rec_hbm, rec_ref), (shapes_hbm, shapes_ref), (elem_hbm, elem_ref),
                (coef_hbm, coef_ref), (first_hbm, first_ref), (bins_hbm, bins_ref),
                (owner_hbm, owner_ref), (second_hbm, second_ref), (turn_hbm, turn_ref),
            )
        )
    ]
    for fetch in fetches:
        fetch.start()

    barrier = pltpu.get_barrier_semaphore()

    partners = [at(x, y, lax.rem(z + dz, 8), core) for dz in (1, 7, 2, 6)]
    for d in (1, 3, 2):
        for pc in range(2):
            partners.append(at(x, lax.rem(y + d, 4), z, pc))
            partners.append(at(lax.rem(x + d, 4), y, z, pc))
    partners.append(at(x, y, z, 1 - core))
    for partner in partners:
        pl.semaphore_signal(barrier, inc=1, device_id=partner, device_id_type=MESH)

    lane128 = lax.broadcasted_iota(i32, (1, 128), 1)
    left = lane128 < HALF

    def swap(tile):
        return pltpu.roll(tile, HALF, 1)

    pad_rec[...] = jnp.zeros_like(pad_rec)
    fetches[0].wait()
    pad_rec[0:HALF, 0:MODES] = rec_ref[...].astype(f32)
    turned = pad_rec[...].T
    gathered[0] = (turned[0:FOLD] + swap(turned[FOLD : 2 * FOLD])).astype(bf16)

    shapes_out[MODES - 12 : 304, :] = jnp.zeros((16, E_DEV), bf16)
    for fetch in fetches[1:4]:
        fetch.wait()
    shapes_out[0:MODES, :] = shapes_ref[...]
    slots = pl.ds(pl.multiple_of(z_half * 128, 128), 128)
    elems = elem_ref[:, slots]
    coefs = coef_ref[:, slots]
    elem_ids = lax.broadcasted_iota(i32, (E_DEV, 128), 0)
    hot = jnp.zeros((304, 128), f32)
    for k in range(K_EXT):
        pick = (elem_ids == elems[k : k + 1, :]).astype(f32).astype(bf16)
        hot = hot + coefs[k : k + 1, :] * jnp.dot(
            shapes_out[...], pick, preferred_element_type=f32
        )
    hot = jnp.concatenate([hot, jnp.zeros((80, 128), f32)], axis=0).T
    for t in range(3):
        c_rows[t * 128 : t * 128 + 128, :] = hot[:, t * 128 : t * 128 + 128]

    for g in range(8):
        for t in range(3):
            for rank in range(2):
                start = t * 128 + z_odd * HALF + 16 * (g // 2) + 2 * (g % 2) + rank
                to = (g * 3 + t) * 8 + rank * 4
                c_out[to : to + 4, :] = c_rows[pl.ds(start, 4, stride=4), :]

    for fetch in fetches[5:]:
        fetch.wait()
    owner_row = owner_ref[...]
    r32 = lax.broadcasted_iota(i32, (32, 32), 0)
    c32 = lax.broadcasted_iota(i32, (32, 32), 1)
    owners = jnp.broadcast_to(owner_row, (32, 32))
    owner_col = jnp.sum(jnp.where(r32 == c32, owners, 0), axis=1, keepdims=True)
    rank = jnp.sum(
        jnp.logical_and(owners == owner_col, c32 < r32).astype(i32), axis=1, keepdims=True
    )
    slot = lax.broadcasted_iota(i32, (32, 64), 1)
    region_x = lax.rem(x + lax.rem(lax.div(slot, 2), 4), 4)
    region_y = lax.rem(y + lax.div(slot, 16), 4)
    region_c = lax.rem(core + lax.rem(slot, 2), 2)
    region = (region_x * 4 + region_y) * 2 + region_c
    chosen = jnp.logical_and(region == owner_col, lax.rem(lax.div(slot, 8), 2) == rank)
    chosen = chosen.astype(f32).astype(bf16)
    pl.semaphore_wait(barrier, len(partners))

    copies = []

    first_rows, last_rows = pl.ds(0, SPLIT), pl.ds(SPLIT, FOLD - SPLIT)

    def a_wait_first(q, j):
        wait(gathered.at[q * 4 + j, first_rows], g_rs.at[q * 4 + j])

    def a_wait_last(q, j):
        wait(gathered.at[q * 4 + j, last_rows], h_rs.at[q * 4 + j])

    def v_send(q):
        for j in (2, 1, 3):
            copies.append(
                send(
                    gathered.at[q * 4, first_rows], gathered.at[q * 4 + j, first_rows],
                    g_ss.at[3 * q + j - 1], g_rs.at[q * 4 + j],
                    line(core, u, lax.rem(v + 4 - j, 4), z, core),
                )
            )

    def z_send(n, q, dq, dz, rows=None):
        src, dst = gathered.at[q * 4, first_rows], gathered.at[dq * 4, first_rows]
        rs = g_rs.at[dq * 4]
        if rows is not None:
            part = pl.ds(rows * (SPLIT // 2), SPLIT // 2)
            src, dst, rs = gathered.at[q * 4, part], gathered.at[dq * 4, part], far_rs.at[rows]
        copies.append(send(src, dst, z_ss.at[n], rs, at(x, y, lax.rem(z + 8 + dz, 8), core)))

    def last_v_send():
        for j in (2, 1, 3):
            copies.append(
                send(
                    gathered.at[0, last_rows], gathered.at[j, last_rows], h_ss.at[j - 1],
                    h_rs.at[j], line(core, u, lax.rem(v + 4 - j, 4), z, core),
                )
            )

    last_count = [3]

    def last_z_send(dz, to, j):
        q, dq = PLANE_AT[dz % 8], PLANE_AT[(dz - to) % 8]
        n = last_count[0]
        last_count[0] += 1
        copies.append(
            send(
                gathered.at[q * 4 + j, last_rows], gathered.at[dq * 4 + j, last_rows], h_ss.at[n],
                h_rs.at[dq * 4 + j], at(x, y, lax.rem(z + 8 + to, 8), core),
            )
        )

    def last_near(j):
        for to in (1, -1, 2, -2):
            last_z_send(0, to, j)

    def last_far(j):
        a_wait_last(PLANE_AT[2], j)
        last_z_send(2, -1, j)
        if j in (0, 1):
            last_z_send(2, -2, j)
        a_wait_last(PLANE_AT[6], j)
        last_z_send(-2, 1, j)
        if j in (2, 3):
            last_z_send(-2, 2, j)

    def group(px, pc):
        return pl.ds(pl.multiple_of(24 * (px * 2 + pc), 8), 24)

    for dx in (2, 1, 3, 0):
        for dc in range(2):
            to_x, to_c = lax.rem(x + dx, 4), jnp.where(dc == 0, core, 1 - core)
            if dx or dc:
                g = ((4 - dx) % 4) * 2 + dc
                send(
                    c_out.at[group(to_x, to_c)], c_mid.at[pl.ds(24 * g, 24)], c1_ss, c1_rs,
                    at(to_x, y, z, to_c),
                )
    c_mid[0:24, :] = c_out[group(x, core), :]

    for n, dz in enumerate((1, 7, 2, 6)):
        z_send(n, 0, PLANE_AT[dz], -dz)
    last_v_send()
    last_near(0)
    v_send(0)

    def c_pass():
        wait(c_mid.at[pl.ds(24, 168)], c1_rs)
        for dy in (2, 1, 3, 0):
            to_y = lax.rem(y + dy, 4)
            for t in range(3):
                for rank in range(2):
                    to = dy * 48 + t * 16 + rank * 8
                    c_next[to : to + 8, :] = c_mid[
                        pl.ds(t * 8 + rank * 4 + to_y, 8, stride=24), :
                    ]
            if dy:
                send(
                    c_next.at[pl.ds(dy * 48, 48)], c_flat.at[pl.ds((4 - dy) * 48, 48)], c2_ss,
                    c2_rs, at(x, to_y, z, core),
                )
        c_flat[0:48, :] = c_next[0:48, :]

    owns = core == z_odd
    shp_to = [
        line(0, lax.rem(x + 4 - z_half, 4), y, z, 0),
        line(1, lax.rem(y + 4 - z_half, 4), x, z, 1),
    ]

    def shape_copies(act):
        for cc in range(2):
            own_work = jnp.logical_and(z_half == 0, core == cc)

            @pl.when(jnp.logical_and(owns, jnp.logical_not(own_work)))
            def _():
                act(
                    pltpu.make_async_remote_copy(
                        src_ref=shapes_out, dst_ref=shapes_in, send_sem=shp_ss.at[cc],
                        recv_sem=shp_rs, device_id=shp_to[cc], device_id_type=MESH,
                    )
                )

    shape_copies(lambda copy: copy.start())
    local_shapes = jnp.logical_and(owns, z_half == 0)

    @pl.when(local_shapes)
    def _():
        shapes_in[...] = shapes_out[...]

    col = lax.broadcasted_iota(i32, (128, 128), 1)
    row = lax.broadcasted_iota(i32, (128, 128), 0)
    source, place, dv = lax.div(col, 32), lax.div(lax.rem(col, 32), 4), lax.rem(col, 4)
    dz = jnp.zeros_like(col)
    for i, value in enumerate(PLANES):
        dz = jnp.where(place == i, value, dz)
    zz = lax.rem(z + dz, 8)
    a_even = 16 * zz + 4 * lax.rem(x + source, 4) + lax.rem(y + dv, 4)
    a_odd = 16 * zz + 4 * lax.rem(x + dv, 4) + lax.rem(y + source, 4)
    fetches[4].wait()
    for half, a_of in enumerate((a_even, a_odd)):
        order = (row == a_of).astype(f32).astype(bf16)
        table[half] = jnp.dot(first_ref[...], order, preferred_element_type=f32).astype(bf16)

    bins = bins_ref[...].astype(f32)
    before = (
        lax.broadcasted_iota(i32, (NB, NB), 0) < lax.broadcasted_iota(i32, (NB, NB), 1)
    ).astype(f32).astype(bf16)
    starts = jnp.dot(
        jnp.broadcast_to(bins, (8, NB)).astype(bf16), before, preferred_element_type=f32
    )[0:1]
    starts_i = starts.astype(i32)
    ends_i = (starts + bins).astype(i32)

    def member_block(i, _):
        rows = lax.broadcasted_iota(i32, (256, 1), 0)
        bin_ids = i * 4 + lax.div(rows, HALF) + DFT_LEN * lax.rem(rows, HALF)
        inside = jnp.logical_and(bin_ids >= starts_i, bin_ids < ends_i)
        member[pl.ds(pl.multiple_of(i * 256, 256), 256), :] = inside.astype(f32).astype(bf16)
        return 0

    for j in (1, 3, 2):
        a_wait_last(0, j)
        last_near(j)
    c_pass()
    for q in (PLANE_AT[1], PLANE_AT[7]):
        a_wait_first(q, 0)
        v_send(q)
    for n, (dz, step) in enumerate(((2, -1), (6, 1))):
        q = PLANE_AT[dz]
        a_wait_first(q, 0)
        z_send(4 + 2 * n, q, PLANE_AT[(dz - step) % 8], step)
        z_send(5 + 2 * n, q, PLANE_AT[4], 2 * step, n)
        v_send(q)
    last_far(0)
    wait(c_flat.at[pl.ds(48, 144)], c2_rs)
    flat = jnp.concatenate(
        [
            jnp.concatenate(
                [c_flat[e * 48 + t * 16 : e * 48 + t * 16 + 16, :] for e in range(4)], axis=0
            )
            for t in range(3)
        ],
        axis=1,
    )
    high = flat.astype(bf16)
    low = (flat - high.astype(f32)).astype(bf16)
    both = jnp.dot(
        chosen, jnp.concatenate([high, low], axis=1), preferred_element_type=f32
    )
    high, low = both[:, 0:384], both[:, 384:768]
    hot_mine[...] = jnp.concatenate(
        [high[:, 0:256], high[:, 256:384] + swap(low[:, 256:384]), low[:, 0:256]], axis=1
    ).astype(bf16)
    for du in (2, 1, 3):
        for cc in range(2):
            here_u, here_v = (x, y) if cc == 0 else (y, x)
            copies.append(
                send(
                    hot_mine, hot_in.at[du * 2 + core], hot_ss.at[du * 2 + cc],
                    hot_rs.at[du * 2 + core], line(cc, lax.rem(here_u + 4 - du, 4), here_v, z, cc),
                )
            )
    copies.append(
        send(hot_mine, hot_in.at[core], hot_ss.at[0], hot_rs.at[core], at(x, y, z, 1 - core))
    )
    hot_in[core] = hot_mine[...]


    for q in (PLANE_AT[3], PLANE_AT[5]):
        a_wait_first(q, 0)
        v_send(q)
    for n in range(2):
        part = pl.ds(n * (SPLIT // 2), SPLIT // 2)
        wait(gathered.at[PLANE_AT[4] * 4, part], far_rs.at[n])
    v_send(PLANE_AT[4])
    for j in (1, 3, 2):
        last_far(j)
    @pl.when(jnp.logical_not(local_shapes))
    def _():
        wait(shapes_in, shp_rs)

    pad_shapes[0:304, :] = shapes_in[...].astype(f32)
    pad_shapes[304:384, :] = jnp.zeros((80, E_DEV), f32)
    shapes_t[...] = pad_shapes[...].T.astype(bf16)
    e_acc[...] = jnp.zeros_like(e_acc)

    def unfold(q):
        parts = []
        for pair in range(2):
            even = gathered[q * 4 + 2 * pair].astype(f32)
            odd = gathered[q * 4 + 2 * pair + 1].astype(f32)
            parts.append(
                (
                    jnp.where(left, even, swap(odd)).astype(bf16),
                    jnp.where(left, swap(even), odd).astype(bf16),
                )
            )
        first = jnp.concatenate([parts[0][0], parts[1][0]], axis=1)
        last = jnp.concatenate([parts[0][1], parts[1][1]], axis=1)
        wide[q, 0:160, :] = first
        wide[q, 160:320, :] = last
        wide[q, 320:384, :] = last[96:160]
        wide[q, 384:544, :] = first
        wide[q, 544:640, :] = last[0:96]

    def energies(q):
        stress = jnp.dot(shapes_t[...], wide[q, 0:384, :], preferred_element_type=f32)
        squares = stress * stress
        e_acc[...] += squares[:, 0:128] + squares[:, 128:256]

    def series(q):
        out = jnp.dot(
            hot_in[...].reshape(256, 640), wide[q], preferred_element_type=f32
        ).reshape(8, 2, 16, 256)
        for pair in range(2):
            lanes = slice(pair * 128, pair * 128 + 128)
            top = out[:, 0, :, lanes].reshape(128, 128)
            low_half = out[:, 1, :, lanes].reshape(128, 128)
            for n, tile in enumerate(
                (
                    jnp.where(left, top, swap(low_half)),
                    jnp.where(left, swap(top), low_half),
                )
            ):
                folded[pl.ds((q % 4) * 4 + pair * 2 + n, 128, stride=16), :] = tile

    def s_send(piece):
        sending[piece] = folded[...].astype(bf16).reshape(8, 16, 16, 128)
        arrived[core, 0, piece] = sending[piece, core]
        for du in (2, 1, 3):
            for cc in range(2):
                n = du * 2 + cc
                copies.append(
                    send(
                        sending.at[piece, n], arrived.at[core, (4 - du) % 4, piece],
                        s_ss.at[piece, n], s_rs.at[core, (4 - du) % 4, piece],
                        line(core, lax.rem(u + du, 4), v, z, cc),
                    )
                )
        copies.append(
            send(
                sending.at[piece, 1 - core], arrived.at[core, 0, piece], s_ss.at[piece, 0],
                s_rs.at[core, 0, piece], at(x, y, z, 1 - core),
            )
        )

    def planes(piece):
        for q in range(4 * piece, 4 * piece + 4):
            for j in range(4):
                if j:
                    a_wait_first(q, j)
                if q not in (PLANE_AT[0], PLANE_AT[2], PLANE_AT[6]):
                    a_wait_last(q, j)
            unfold(q)
            energies(q)

    planes(0)
    for du in range(1, 4):
        for cc in range(2):
            wait(hot_in.at[du * 2 + cc], hot_rs.at[du * 2 + cc])
    wait(hot_in.at[1 - core], hot_rs.at[1 - core])

    for q in range(4):
        series(q)
    s_send(0)
    planes(1)

    e_mine[0] = jnp.sum(e_acc[...].T, axis=0, keepdims=True)
    e_local = jnp.logical_and(z_half == 0, core == z_odd)
    e_to = line(core, lax.rem(u + z_half, 4), v, z, z_odd)

    def e_first(act):
        @pl.when(jnp.logical_not(e_local))
        def _():
            act(
                pltpu.make_async_remote_copy(
                    src_ref=e_mine, dst_ref=e_in.at[pl.ds(core, 1)], send_sem=e1_ss,
                    recv_sem=e1_rs.at[core], device_id=e_to, device_id_type=MESH,
                )
            )

    e_first(lambda copy: copy.start())

    @pl.when(e_local)
    def _():
        e_in[core] = e_mine[0]

    def a_wait(piece):
        for half in range(2):
            for du in range(1, 4):
                wait(arrived.at[half, du, piece], s_rs.at[half, du, piece])
        wait(arrived.at[1 - core, 0, piece], s_rs.at[1 - core, 0, piece])

    for q in range(4, 8):
        series(q)
    s_send(1)

    def e_slot(d):
        return lax.div(lax.rem(z + d, 8), 2)

    def e_wait(d):
        wait(e_all.at[pl.ds(e_slot(d), 1)], e2_rs.at[e_slot(d)])

    def e_copy(src, d, to, n):
        return pltpu.make_async_remote_copy(
            src_ref=src, dst_ref=e_all.at[pl.ds(e_slot(d), 1)], send_sem=e2_ss.at[n],
            recv_sem=e2_rs.at[e_slot(d)], device_id=at(x, y, lax.rem(z + to, 8), core),
            device_id_type=MESH,
        )

    def e_second(act):
        @pl.when(owns)
        def _():
            for n, to in enumerate((1, 7, 2, 6)):
                act(e_copy(e_sum, 0, to, n))

    def e_third(act):
        @pl.when(owns)
        def _():
            act(e_copy(e_all.at[pl.ds(e_slot(2), 1)], 2, 6, 4))

        @pl.when(jnp.logical_not(owns))
        def _():
            act(e_copy(e_all.at[pl.ds(e_slot(1), 1)], 1, 6, 4))
            act(e_copy(e_all.at[pl.ds(e_slot(7), 1)], 7, 2, 5))

    lax.fori_loop(0, 10, member_block, 0)

    @pl.when(owns)
    def _():
        for cc in range(2):

            @pl.when(jnp.logical_not(jnp.logical_and(z_half == 0, core == cc)))
            def _():
                wait(e_in.at[pl.ds(cc, 1)], e1_rs.at[cc])

        e_sum[0] = e_in[0] + e_in[1]
        e_all[z_half] = e_sum[0]

    e_second(lambda copy: copy.start())
    lax.fori_loop(10, 32, member_block, 0)
    a_wait(0)
    @pl.when(owns)
    def _():
        e_wait(2)

    @pl.when(jnp.logical_not(owns))
    def _():
        e_wait(1)
        e_wait(7)

    e_third(lambda copy: copy.start())

    a_wait(1)
    for pp in range(8):
        ones = []
        for half in range(2):
            tiles = []
            for n in range(2):
                tiles.append(
                    jnp.concatenate(
                        [
                            arrived[half, i, piece, 2 * pp + n]
                            for i in range(4)
                            for piece in range(2)
                        ],
                        axis=0,
                    )
                )
            ones.append(
                jnp.dot(table[half], jnp.concatenate(tiles, axis=1), preferred_element_type=f32)
            )
        for n in range(2):
            lanes = slice(n * 128, n * 128 + 128)
            for half in range(2):
                real, imag = ones[half][0:128, lanes], ones[half][128:256, lanes]
                c, s = turn_ref[2 * half], turn_ref[2 * half + 1]
                rows = slice((2 * pp + n) * 128, (2 * pp + n) * 128 + 128)
                twiddled[rows, half * 256 : half * 256 + 128] = (real * c + imag * s).astype(bf16)
                twiddled[rows, half * 256 + 128 : half * 256 + 256] = (
                    imag * c - real * s
                ).astype(bf16)

    second = second_ref[...].astype(bf16)
    for chunk in range(4):
        out = jnp.dot(
            twiddled[chunk * 512 : chunk * 512 + 512, :], second, preferred_element_type=f32
        )
        real, imag = out[:, 0:128], out[:, 128:256]
        squares = real * real + imag * imag
        for n in range(4):
            power[pl.ds(4 * chunk + n, 128, stride=16), :] = squares[n * 128 : n * 128 + 128]

    sums = jnp.zeros((HS_DEV, NB), f32)
    for kb in range(32):
        tiles = []
        for pair in range(2):
            base = (kb * 4 + pair * 2) * 16
            even, odd = power[base : base + 16, :], power[base + 16 : base + 32, :]
            tiles.append(
                jnp.concatenate(
                    [jnp.where(left, even, swap(odd)), jnp.where(left, swap(even), odd)], axis=0
                )
            )
        sums = sums + jnp.dot(
            jnp.concatenate(tiles, axis=1).astype(bf16),
            member[kb * 256 : kb * 256 + 256, :],
            preferred_element_type=f32,
        )
    band_ref[...] = sums / (NT * bins)

    @pl.when(owns)
    def _():
        e_wait(6)
        e_wait(4)

    @pl.when(jnp.logical_not(owns))
    def _():
        e_wait(3)
        e_wait(5)

    energy_ref[...] = jnp.sqrt(((e_all[0] + e_all[1]) + (e_all[2] + e_all[3])) / NT + epsilon).reshape(E_DEV)

    for copy in copies:
        copy.wait_send()
    wait(c_out.at[pl.ds(24, 168)], c1_ss)
    wait(c_next.at[pl.ds(48, 144)], c2_ss)
    shape_copies(lambda copy: copy.wait_send())
    e_first(lambda copy: copy.wait_send())
    e_second(lambda copy: copy.wait_send())
    e_third(lambda copy: copy.wait_send())


def shards(mode_record, mode_shapes, map_elem, map_coef, hot_owner, band_bins):
    f32, bf16 = jnp.float32, jnp.bfloat16
    first, turn, second = tables()
    vmem, dma = pltpu.VMEM, pltpu.SemaphoreType.DMA
    scratch = [
        vmem((HALF, MODES), bf16),
        vmem((MODES, E_DEV), bf16),
        vmem(map_elem.shape, jnp.int32),
        vmem(map_coef.shape, f32),
        vmem((1, HS_DEV), jnp.int32),
        vmem((1, NB), jnp.int32),
        vmem(first.shape, bf16),
        vmem(turn.shape, f32),
        vmem(second.shape, f32),
        vmem((128, 384), f32),
        vmem((384, 384), f32),
        vmem((304, 384), bf16),
        vmem((304, 384), bf16),
        vmem((384, 384), bf16),
        vmem((384, 128), f32),
        vmem((192, 128), f32),
        vmem((192, 128), f32),
        vmem((192, 128), f32),
        vmem((192, 128), f32),
        vmem((32, 640), bf16),
        vmem((8, 32, 640), bf16),
        vmem((32, FOLD, 128), bf16),
        vmem((8, 640, 256), bf16),
        vmem((2048, 128), f32),
        vmem((2, 8, 16, 16, 128), bf16),
        vmem((2, 4, 2, 16, 16, 128), bf16),
        vmem((NT // 2, NB), bf16),
        vmem((2048, 512), bf16),
        vmem((2048, 128), f32),
        vmem((2, 256, 128), bf16),
        vmem((384, 128), f32),
        vmem((1, 1, 384), f32),
        vmem((2, 1, 384), f32),
        vmem((1, 1, 384), f32),
        vmem((4, 1, 384), f32),
        dma((2,)), dma, dma, dma, dma, dma, dma((8,)), dma((8,)), dma((24,)), dma((32,)), dma((8,)), dma((2,)), dma((31,)), dma((32,)),
        dma((2, 8)), dma((2, 4, 2)), dma, dma((2,)), dma((8,)), dma((4,)),
        dma((9,)),
    ]
    whole = pl.BlockSpec(memory_space=pltpu.VMEM)
    sums, energy = pl.pallas_call(
        kernel,
        out_shape=(
            pltpu.VMEM((HS_DEV, NB), f32),
            pltpu.VMEM((E_DEV,), f32),
        ),
        in_specs=[pl.BlockSpec(memory_space=pltpu.HBM)] * 9,
        out_specs=(whole, whole),
        scratch_shapes=scratch,
        compiler_params=pltpu.CompilerParams(
            collective_id=0, has_side_effects=True, vmem_limit_bytes=255 * 2**18
        ),
        name="whipping",
    )(
        mode_record.T, mode_shapes, map_elem, map_coef, hot_owner.reshape(1, HS_DEV),
        band_bins.reshape(1, NB), jnp.asarray(first), jnp.asarray(turn), jnp.asarray(second),
    )
    return (energy, sums)


def solution(mesh):
    in_specs = (
        P(None, ("ta", "ha")),
        P(None, "ha"),
        P(None, "ha"),
        P(None, "ha"),
        P(("ta", "ha")),
        P(),
    )
    out_specs = (P("ha"), P(("ta", "ha"), None))
    return jax.shard_map(shards, mesh=mesh, in_specs=in_specs, out_specs=out_specs, check_vma=False)
```
